256 devices in a mesh: pipe: 4 (over z_hi), row: 8 (over z_lo, x), col: 8 (over y, core).
Axes of the slice: x: 4, y: 4, z: 8 (z_hi: 4, z_lo: 2; z = z_hi * 2 + z_lo), core: 2. Of those that a mesh axis runs over, the one named last changes fastest.
Arguments:
- inputs: bfloat16 [4, 2, 512, 4096], P('pipe', None, 'col', 'row'), may hold values from -120 to 120
- grad_out: bfloat16 [2, 512, 4096], P(None, 'col', 'row'), may hold values from -6 to 6
- norm_gain: bfloat16 [4, 4096], P('pipe', 'row'), may hold values from 0.5 to 2
- gate_weight: bfloat16 [4, 4096, 2048], P('pipe', 'col', 'row'), may hold values from -0.25 to 0.25
- up_weight: bfloat16 [4, 4096, 2048], P('pipe', 'col', 'row'), may hold values from -0.25 to 0.25
- down_weight: bfloat16 [4, 4096, 2048], P('pipe', 'col', 'row'), may hold values from -0.25 to 0.25
- inner_cols: int32 [4, 32, 16], P('pipe', None, 'row'), may hold values from 0 to 13, as said below
- inner_counts: int32 [4, 32, 8], P('pipe', None, 'row'), may hold values from 1 to 2, as said below
- outer_cols: int32 [4, 32, 16], P('pipe', None, 'row'), may hold values from 0 to 13, as said below
- outer_counts: int32 [4, 32, 8], P('pipe', None, 'row'), may hold values from 1 to 2, as said below
Outputs:
- grad_in: bfloat16 [4, 2, 512, 4096], P('pipe', None, 'col', 'row')
- grad_gate: bfloat16 [4, 4096, 2048], P('pipe', 'col', 'row')
- grad_up: bfloat16 [4, 4096, 2048], P('pipe', 'col', 'row')
- grad_down: bfloat16 [4, 4096, 2048], P('pipe', 'col', 'row')
The draws below stay inside these ranges and needn't reach their ends.
Inputs may be any that keep to these rules, and one draw needn't show every extreme that they name: `inner_cols`: within each group of 2 slots of a block row the entries are distinct. `inner_counts`: a slot s of a group is live when s is below the count. `outer_cols`: within each group of 2 slots of a block row the entries are distinct. `outer_counts`: a slot s of a group is live when s is below the count.
All inputs are finite; a program needn't handle non-finite values.
Results may differ from the reference program's by a relative error of at most 0.017.
Values may be sent and summed in bfloat16 or wider, within the bound.
A program may use at most 256 MiB of HBM per device.

```python
import math
import jax
import jax.numpy as jnp
from jax import lax

D = 4096
FF = 14336
BLK = 128
M = 2
TOKENS = 512
LCB = 14
CAP = 2
SLOTS = 2048
N_PIPE = 4
N_ROW = 8


def draw_inputs(key, part):
    key_base, key_rows, key_cols = jax.random.split(key, 3)
    shape = (N_PIPE, M, TOKENS, D)
    feature = jnp.arange(D, dtype=jnp.float32) / D
    base = jnp.clip(jax.random.normal(key_base, shape, jnp.float32), -4.0, 4.0)
    row_scale = jnp.exp(jax.random.uniform(key_rows, (N_PIPE, M, TOKENS, 1), jnp.float32, math.log(0.3), math.log(3.0)))
    col_scale = (1.0 + 2.0 * feature) * jnp.exp(jax.random.uniform(key_cols, (D,), jnp.float32, -0.35, 0.35))
    return (base * row_scale * col_scale).astype(jnp.bfloat16)


def block_columns(key):
    shape = (N_PIPE, D // BLK, N_ROW, LCB)
    raw_scores = jax.random.randint(key, shape, 0, 1 << 20, dtype=jnp.int32)
    scores = raw_scores * LCB + jnp.arange(LCB, dtype=jnp.int32)
    scores = scores.at[:, 0, :, LCB - 1].set(-2)
    scores = scores.at[:, 1, :, 0].set(-2)
    ordered = jnp.argsort(scores, axis=-1, stable=True)[..., :CAP]
    return ordered.reshape(N_PIPE, D // BLK, N_ROW * CAP).astype(jnp.int32)


def block_counts(key):
    counts = jax.random.randint(key, (N_PIPE, D // BLK, N_ROW), 1, CAP + 1, dtype=jnp.int32)
    counts = counts.at[:, 0, :].set(CAP)
    counts = counts.at[:, 1, :].set(1)
    return counts.astype(jnp.int32)


def draw_inner_cols(key, part):
    return block_columns(jax.random.fold_in(key, 11))


def draw_outer_cols(key, part):
    return block_columns(jax.random.fold_in(key, 12))


def draw_inner_counts(key, part):
    return block_counts(jax.random.fold_in(key, 21))


def draw_outer_counts(key, part):
    return block_counts(jax.random.fold_in(key, 22))


def block_scale(key, dims, shards, least, largest):
    factor_of = 1.0
    for position, parts in shards:
        heights = jax.random.uniform(jax.random.fold_in(jax.random.fold_in(key, 6), position), (parts,), jnp.float32, least / len(shards), largest / len(shards))
        factor_of = factor_of * jnp.repeat(jnp.exp(heights), dims[position] // parts).reshape((-1,) + (1,) * (len(dims) - 1 - position))
    return factor_of


def gaussian(rng, extent, scale, bound, pieces=(), held_as=jnp.bfloat16):
    drawn = jax.random.normal(rng, extent, jnp.float32) * scale
    if len(pieces) > 0:
        drawn = block_scale(rng, extent, pieces, -0.22, 0.18) * drawn
    return jnp.clip(drawn, min=-bound, max=bound).astype(held_as)


def setup_inputs(seed: int = 0) -> dict:
    keys = jax.random.split(jax.random.key(seed), 11)
    return {
        "inputs": draw_inputs(jax.random.fold_in(keys[10], 71), 0),
        "grad_out": gaussian(keys[1], (M, TOKENS, D), 1.0, 6.0, ((1, 8), (2, 8))),
        "norm_gain": jnp.clip(jnp.exp(math.log(2.0) - 1.3862944 * jax.random.uniform(keys[2], (N_PIPE, D), jnp.float32) ** block_scale(keys[2], (N_PIPE, D), ((0, 4), (1, 8)), -0.2, 0.2)), 0.5, 2.0).astype(jnp.bfloat16),
        "gate_weight": gaussian(keys[3], (N_PIPE, D, SLOTS), (D * (CAP + 1) // (2 * LCB)) ** -0.5, 0.25, ((0, 4), (1, 8), (2, 8))),
        "up_weight": gaussian(keys[4], (N_PIPE, D, SLOTS), (D * (CAP + 1) // (2 * LCB)) ** -0.5, 0.25, ((0, 4), (1, 8), (2, 8))),
        "down_weight": gaussian(keys[5], (N_PIPE, D, SLOTS), (D * (CAP + 1) // (2 * LCB)) ** -0.5, 0.25, ((0, 4), (1, 8), (2, 8))),
        "inner_cols": draw_inner_cols(jax.random.fold_in(keys[10], 71), 0),
        "inner_counts": draw_inner_counts(jax.random.fold_in(keys[10], 71), 0),
        "outer_cols": draw_outer_cols(jax.random.fold_in(keys[10], 71), 0),
        "outer_counts": draw_outer_counts(jax.random.fold_in(keys[10], 71), 0),
    }


EPSILON = 1e-05
HIGHEST = lax.Precision.HIGHEST

def unpack_blocks(weight, columns, counts):
    block_rows = D // BLK
    slot_total = N_ROW * CAP
    shaped = weight.astype(jnp.float32).reshape(block_rows, BLK, slot_total, BLK)
    slot_ids = jnp.arange(slot_total, dtype=jnp.int32)
    group_ids = slot_ids // CAP
    global_cols = (group_ids[None, :] * LCB + columns).astype(jnp.int32)
    live_slots = ((slot_ids % CAP)[None, :] < counts[:, group_ids]).astype(jnp.float32)
    return (shaped * live_slots[:, None, :, None], global_cols, live_slots)

def spread_blocks(activation, blocks, global_cols):
    row_count = activation.shape[0]
    block_rows = blocks.shape[0]
    shaped = activation.astype(jnp.float32).reshape(row_count, block_rows, BLK)
    product = jnp.einsum('trk,rksn->trsn', shaped, blocks, precision=HIGHEST)
    result = jnp.zeros((row_count, FF // BLK, BLK), jnp.float32).at[:, global_cols].add(product)
    return result.reshape(row_count, FF)

def pick_blocks(values, global_cols):
    row_count = values.shape[0]
    return values.astype(jnp.float32).reshape(row_count, FF // BLK, BLK)[:, global_cols]

def gather_back(picked, blocks):
    result = jnp.einsum('trsn,rksn->trk', picked, blocks, precision=HIGHEST)
    return result.reshape(picked.shape[0], D)

def weight_term(activation, picked, live_slots):
    row_count = activation.shape[0]
    block_rows = picked.shape[1]
    shaped = activation.astype(jnp.float32).reshape(row_count, block_rows, BLK)
    result = jnp.einsum('trk,trsn->rksn', shaped, picked, precision=HIGHEST)
    return result * live_slots[:, None, :, None]

def reference(inputs, grad_out, norm_gain, gate_weight, up_weight, down_weight, inner_cols, inner_counts, outer_cols, outer_counts):
    grads_in = [None] * N_PIPE
    gate_grads = [None] * N_PIPE
    up_grads = [None] * N_PIPE
    down_grads = [None] * N_PIPE
    incoming = grad_out
    for phase in reversed(range(N_PIPE)):
        gate_blocks, inner_global, inner_live = unpack_blocks(gate_weight[phase], inner_cols[phase], inner_counts[phase])
        up_blocks, _, _ = unpack_blocks(up_weight[phase], inner_cols[phase], inner_counts[phase])
        down_blocks, outer_global, outer_live = unpack_blocks(down_weight[phase], outer_cols[phase], outer_counts[phase])
        inputs_full = inputs[phase].astype(jnp.float32)
        gain_full = norm_gain[phase].astype(jnp.float32)
        inverse_rms = lax.rsqrt(lax.optimization_barrier(jnp.mean(inputs_full * inputs_full, axis=2)) + EPSILON)
        normed = (inputs_full * inverse_rms[:, :, None] * gain_full).astype(jnp.bfloat16)
        shape_term = gate_blocks.shape
        sum_gate = jnp.zeros(shape_term, jnp.float32)
        sum_up = jnp.zeros(shape_term, jnp.float32)
        sum_down = jnp.zeros(shape_term, jnp.float32)
        results = []
        for batch_index in range(M):
            grad_now = incoming[batch_index]
            normed_now = normed[batch_index]
            gate_pre = spread_blocks(normed_now, gate_blocks, inner_global)
            up_pre = spread_blocks(normed_now, up_blocks, inner_global)
            grad_hidden = spread_blocks(grad_now, down_blocks, outer_global)
            sigmoid = jax.nn.sigmoid(gate_pre)
            hidden = (gate_pre * sigmoid * up_pre).astype(jnp.bfloat16)
            grad_gate_now = (grad_hidden * up_pre * sigmoid * (1.0 + gate_pre * (1.0 - sigmoid))).astype(jnp.bfloat16)
            grad_up_now = (grad_hidden * gate_pre * sigmoid).astype(jnp.bfloat16)
            picked_gate = pick_blocks(grad_gate_now, inner_global)
            picked_up = pick_blocks(grad_up_now, inner_global)
            partial_sum = gather_back(picked_gate, gate_blocks) + gather_back(picked_up, up_blocks)
            full_now = inputs_full[batch_index]
            inverse_now = inverse_rms[batch_index]
            statistic = lax.optimization_barrier(jnp.sum(full_now * gain_full * partial_sum, axis=1))
            result = grad_now.astype(jnp.float32) + gain_full * inverse_now[:, None] * partial_sum
            result = result - full_now * (inverse_now ** 3 * statistic / D)[:, None]
            results.append(result.astype(jnp.bfloat16))
            sum_down = sum_down + weight_term(grad_now, pick_blocks(hidden, outer_global), outer_live)
            sum_gate = sum_gate + weight_term(normed_now, picked_gate, inner_live)
            sum_up = sum_up + weight_term(normed_now, picked_up, inner_live)
        incoming = jnp.stack(results)
        grads_in[phase] = incoming
        gate_grads[phase] = sum_gate.reshape(D, N_ROW * CAP * BLK).astype(jnp.bfloat16)
        up_grads[phase] = sum_up.reshape(D, N_ROW * CAP * BLK).astype(jnp.bfloat16)
        down_grads[phase] = sum_down.reshape(D, N_ROW * CAP * BLK).astype(jnp.bfloat16)
    return (jnp.stack(grads_in), jnp.stack(gate_grads), jnp.stack(up_grads), jnp.stack(down_grads))
```

```python
import functools

import jax
import jax.numpy as jnp
from jax import lax
from jax.experimental import pallas as pl
from jax.experimental.pallas import tpu as pltpu
from jax.sharding import PartitionSpec as P

FF = 14336
BLK = 128
EPSILON = 1e-05
MESH = pl.DeviceIdType.MESH
F32 = jnp.float32
BF16 = jnp.bfloat16


def sort_kernel(blocks, icol, ocol, iord, ikeep, iend, ihas, oord, okeep, oend, ohas, start):
    slots = icol.shape[0]
    for col, order, keep, end, has in ((icol, iord, ikeep, iend, ihas), (ocol, oord, okeep, oend, ohas)):

        def clear(j, _):
            start[j] = 0
            return 0

        lax.fori_loop(0, blocks + 1, clear, 0)

        def count(k, _, col=col):
            start[col[k] + 1] = start[col[k] + 1] + 1
            return 0

        lax.fori_loop(0, slots, count, 0)

        def total(j, _, has=has):
            has[j] = jnp.minimum(start[j + 1], 1).astype(F32)
            start[j + 1] = start[j + 1] + start[j]
            return 0

        lax.fori_loop(0, blocks, total, 0)

        def place(k, _, col=col, order=order, end=end):
            at = start[col[k]]
            order[at] = k
            start[col[k]] = at + 1
            end[col[k]] = at
            return 0

        def last(j, _, end=end):
            end[j] = 0
            return 0

        lax.fori_loop(0, blocks, last, 0)
        lax.fori_loop(0, slots, place, 0)
        keep[0] = 0.0

        def same(i, _, col=col, order=order, keep=keep):
            keep[i] = jnp.where(col[order[i]] == col[order[i - 1]], 1.0, 0.0).astype(F32)
            return 0

        lax.fori_loop(1, slots, same, 0)


def dot(a, b):
    return jnp.dot(a, b, preferred_element_type=F32)


def dot_nt(a, b):
    return lax.dot_general(a, b, (((1,), (1,)), ((), ())), preferred_element_type=F32)


def main_kernel(
    sizes,
    x_ref, go_ref, gain_ref, gate_ref, up_ref, down_ref,
    icol, icnt, ocol, ocnt,
    iord, ikeep, iend, ihas, oord, okeep, oend, ohas,
    gin_ref, ggate_ref, gup_ref, gdown_ref,
    wall, xg, xn, xnt, rinv, pg, pu, sg, su, ab, bb, cb, hb, dgb, dub, dyg, rss, rsr, ds, dr, ys, yr, own,
    wsend, wrecv, xsend, xrecv, gsend, grecv, hsend, hrecv, rsend, rrecv, dsend, drecv, ysend, yrecv,
):
    n_pipe, n_row, n_y, blocks = sizes
    micro, tokens, width = go_ref.shape
    both = micro * tokens
    features = width * n_row
    block_rows = features // BLK
    per_row = block_rows // n_row
    per_col = block_rows // (2 * n_y)
    slots = 2 * block_rows
    half = per_col * 3 * BLK // 2

    p = lax.axis_index("pipe")
    r = lax.axis_index("row")
    c = lax.axis_index("col")
    y = lax.div(c, 2)
    core = lax.rem(c, 2)

    def column(dy, dcore):
        return lax.rem(y + dy, n_y) * 2 + lax.rem(core + dcore, 2)

    up_y, down_y, far_y, sibling = column(1, 0), column(n_y - 1, 0), column(2, 0), column(0, 1)

    def rows_of(block, which):
        return pl.ds((block * 3 + which) * BLK, BLK)

    barrier = pltpu.get_barrier_semaphore()

    def greet(d, _):
        pl.semaphore_signal(barrier, inc=1, device_id={"row": lax.rem(r + d, n_row)}, device_id_type=MESH)
        return 0

    lax.fori_loop(1, n_row, greet, 0)
    for other in (up_y, down_y, far_y, sibling):
        pl.semaphore_signal(barrier, inc=1, device_id={"col": other}, device_id_type=MESH)

    @pl.when(p > 0)
    def _():
        pl.semaphore_signal(barrier, inc=1, device_id={"pipe": p - 1}, device_id_type=MESH)

    @pl.when(p < n_pipe - 1)
    def _():
        pl.semaphore_signal(barrier, inc=1, device_id={"pipe": p + 1}, device_id_type=MESH)

    xg[r, 0:both, :] = x_ref[...]
    xg[r, both : both + 16, :] = jnp.broadcast_to(gain_ref[...].astype(F32), (16, width)).astype(BF16)
    for i in range(per_col):
        for which, (ref, cnt) in enumerate(((gate_ref, icnt), (up_ref, icnt), (down_ref, ocnt))):
            live = cnt[c * per_col + i]
            shape = (BLK, 2 * BLK)
            slot = lax.broadcasted_iota(jnp.int32, shape, 1) // BLK
            value = ref[i * BLK : (i + 1) * BLK, :].astype(F32)
            wall[c, rows_of(i, which), :] = jnp.where(slot < live, value, 0.0).astype(BF16)

    @pl.when(p == n_pipe - 1)
    def _():
        for m in range(micro):
            dyg[m, r] = go_ref[m]

    pl.semaphore_wait(barrier, n_row + 3 + jnp.where(p > 0, 1, 0) + jnp.where(p < n_pipe - 1, 1, 0))

    def weights(owner, h, target, number):
        piece = wall.at[owner, pl.ds(h * half, half), :]
        return pltpu.make_async_remote_copy(
            src_ref=piece, dst_ref=piece, send_sem=wsend.at[number], recv_sem=wrecv.at[owner, h],
            device_id={"col": target}, device_id_type=MESH,
        )

    def x_copy(owner, target, number):
        return pltpu.make_async_remote_copy(
            src_ref=xg.at[owner], dst_ref=xg.at[owner], send_sem=xsend.at[number], recv_sem=xrecv.at[owner],
            device_id={"row": target}, device_id_type=MESH,
        )

    def dy_copy(m, owner, target, number):
        piece = dyg.at[m, owner]
        return pltpu.make_async_remote_copy(
            src_ref=piece, dst_ref=piece, send_sem=gsend.at[m, number], recv_sem=grecv.at[m, owner],
            device_id={"row": target}, device_id_type=MESH,
        )

    def hop_copy(m, target):
        return pltpu.make_async_remote_copy(
            src_ref=gin_ref.at[m], dst_ref=dyg.at[m, r], send_sem=hsend.at[m], recv_sem=hrecv.at[m],
            device_id={"pipe": target}, device_id_type=MESH,
        )

    def sum_copy(m, target, source, number):
        return pltpu.make_async_remote_copy(
            src_ref=rss.at[m, target], dst_ref=rsr.at[m, source], send_sem=rsend.at[m, number], recv_sem=rrecv.at[m, source],
            device_id={"row": target}, device_id_type=MESH,
        )

    def pair_copy(which, k):
        return pltpu.make_async_remote_copy(
            src_ref=ds.at[which, k], dst_ref=dr.at[which, k], send_sem=dsend.at[which, k], recv_sem=drecv.at[which, k],
            device_id={"col": sibling}, device_id_type=MESH,
        )

    def ring_copy(which, k, target):
        return pltpu.make_async_remote_copy(
            src_ref=ys.at[which, k], dst_ref=yr.at[which, k], send_sem=ysend.at[which, k], recv_sem=yrecv.at[which, k],
            device_id={"col": target}, device_id_type=MESH,
        )

    def send_dy(m):
        def body(d, _):
            dy_copy(m, r, lax.rem(r + d, n_row), d).start()
            return 0

        lax.fori_loop(1, n_row, body, 0)

    def send_x(d, _):
        x_copy(r, lax.rem(r + d, n_row), d).start()
        return 0

    lax.fori_loop(1, n_row, send_x, 0)
    weights(c, 0, up_y, 0).start()
    weights(c, 1, down_y, 1).start()
    weights(c, 1, up_y, 2).start()
    weights(c, 0, down_y, 3).start()
    weights(c, 0, sibling, 4).start()
    weights(c, 1, sibling, 5).start()

    @pl.when(p == n_pipe - 1)
    def _():
        for m in range(micro):
            send_dy(m)

    rinv[...] = jnp.zeros_like(rinv)

    def squares(d, _):
        owner = lax.rem(r + d, n_row)

        @pl.when(d > 0)
        def _():
            x_copy(owner, owner, 0).wait_recv()

        total = rinv[...]
        for i in range(per_row):
            value = xg[owner, 0:both, i * BLK : (i + 1) * BLK].astype(F32)
            total = total + value * value
        rinv[...] = total
        return 0

    lax.fori_loop(0, n_row, squares, 0)
    mean = jnp.sum(rinv[...], axis=1, keepdims=True) / features
    rinv[...] = jnp.broadcast_to(lax.rsqrt(mean + EPSILON), (both, BLK))

    def norm(owner, _):
        scale = rinv[...]
        for i in range(per_row):
            lanes = slice(i * BLK, (i + 1) * BLK)
            gain = xg[owner, both : both + 16, lanes].astype(F32)[0:1, :]
            value = xg[owner, 0:both, lanes].astype(F32)
            xn[owner * per_row + i] = (value * scale * gain).astype(BF16)
        return 0

    lax.fori_loop(0, n_row, norm, 0)

    def arrive(k, _):
        @pl.when(k == 1)
        def _():
            for h in range(2):
                weights(sibling, h, sibling, 0).wait_recv()

        @pl.when(k == 2)
        def _():
            weights(down_y, 0, sibling, 0).wait_recv()
            weights(down_y, 0, up_y, 6).start()
            weights(down_y, 0, sibling, 7).start()
            weights(up_y, 1, sibling, 0).wait_recv()
            weights(up_y, 1, down_y, 8).start()
            weights(up_y, 1, sibling, 9).start()
            weights(down_y, 1, sibling, 0).wait_recv()
            weights(down_y, 1, sibling, 10).start()

        @pl.when(k == 3)
        def _():
            weights(up_y, 0, sibling, 0).wait_recv()
            weights(up_y, 0, sibling, 11).start()

        @pl.when(k == 4)
        def _():
            for h in range(2):
                weights(column(n_y - 1, 1), h, sibling, 0).wait_recv()

        @pl.when(k == 5)
        def _():
            for h in range(2):
                weights(column(1, 1), h, sibling, 0).wait_recv()

        @pl.when(k == 6)
        def _():
            for h in range(2):
                weights(far_y, h, sibling, 0).wait_recv()
                weights(far_y, h, sibling, 12 + h).start()

        @pl.when(k == 7)
        def _():
            for h in range(2):
                weights(column(2, 1), h, sibling, 0).wait_recv()

        turn = jnp.where(k < 2, 0, jnp.where(k >= 6, 2, jnp.where(lax.rem(k, 2) == 0, n_y - 1, 1)))
        other = jnp.where(jnp.logical_or(k == 1, jnp.logical_or(k == 4, jnp.logical_or(k == 5, k == 7))), 1, 0)
        owner = column(turn, other)
        for i in range(per_col):
            block_row = owner * per_col + i
            value = xn[block_row]
            for which, out in ((0, pg), (1, pu)):
                product = dot(value, wall[owner, rows_of(i, which), :])
                out[2 * block_row] = product[:, :BLK]
                out[2 * block_row + 1] = product[:, BLK:]
        return 0

    lax.fori_loop(0, 2 * n_y, arrive, 0)

    def add_slots(order, keep, source, out, rows):
        def body(i, total):
            total = total * keep[i] + source[order[i], 0:rows, :]
            out[i, 0:rows, :] = total
            return total

        lax.fori_loop(0, slots, body, jnp.zeros((rows, BLK), F32), unroll=4)

    add_slots(iord, ikeep, pg, sg, both)
    add_slots(iord, ikeep, pu, su, both)

    def hidden(j, _):
        g = sg[iend[j]] * ihas[j]
        u = su[iend[j]] * ihas[j]
        s = jax.nn.sigmoid(g)
        a = u * s * (1.0 + g * (1.0 - s))
        b = g * s
        h = (b * u).astype(BF16)
        e = a * g + b * u
        for m in range(micro):
            part = slice(m * tokens, (m + 1) * tokens)
            ab[m, j] = a[part]
            bb[m, j] = b[part]
            cb[m, j] = e[part]
            hb[m, j] = h[part]
        return 0

    lax.fori_loop(0, blocks, hidden, 0)

    def stacked(ref, j):
        return jnp.concatenate([ref[m, j] for m in range(micro)], axis=0)

    def grads(owner, emit):
        for i in range(per_col):
            block_row = owner * per_col + i
            row_owner = lax.div(block_row, per_row)
            place = lax.rem(block_row, per_row)
            rows = slice(i * BLK, (i + 1) * BLK)
            j0, j1 = icol[2 * block_row], icol[2 * block_row + 1]
            q0, q1 = ocol[2 * block_row], ocol[2 * block_row + 1]
            lanes = pl.ds(pl.multiple_of(place * BLK, BLK), BLK)
            dy = jnp.concatenate([dyg[m, row_owner, :, lanes] for m in range(micro)], axis=0)
            emit(2, rows, dot(dy.T, jnp.concatenate([stacked(hb, q0), stacked(hb, q1)], axis=1)))
            left = xnt[block_row]
            emit(0, rows, dot(left, jnp.concatenate([stacked(dgb, j0), stacked(dgb, j1)], axis=1)))
            emit(1, rows, dot(left, jnp.concatenate([stacked(dub, j0), stacked(dub, j1)], axis=1)))

    def grads_sibling():
        def body(k, _):
            def emit(which, rows, value):
                ds[which, k, rows, :] = value.astype(BF16)

            grads(lax.rem(y + k, n_y) * 2 + (1 - core), emit)
            for which in range(3):
                pair_copy(which, k).start()
            return 0

        lax.fori_loop(0, n_y, body, 0)

    def front(m):
        def products(d, _):
            owner = lax.rem(r + d, n_row)

            @pl.when(d > 0)
            def _():
                dy_copy(m, owner, owner, 0).wait_recv()

            for i in range(per_row):
                block_row = owner * per_row + i
                col_owner = lax.div(block_row, per_col)
                place = lax.rem(block_row, per_col)
                rows = pl.ds(pl.multiple_of((place * 3 + 2) * BLK, BLK), BLK)
                product = dot(dyg[m, owner, :, i * BLK : (i + 1) * BLK], wall[col_owner, rows, :])
                pg[2 * block_row, 0:tokens, :] = product[:, :BLK]
                pg[2 * block_row + 1, 0:tokens, :] = product[:, BLK:]
            return 0

        lax.fori_loop(0, n_row, products, 0)
        add_slots(oord, okeep, pg, sg, tokens)

        def gated(j, total):
            dh = sg[oend[j], 0:tokens, :] * ohas[j]
            dgb[m, j] = (dh * ab[m, j]).astype(BF16)
            dub[m, j] = (dh * bb[m, j]).astype(BF16)
            return total + dh * cb[m, j]

        total = lax.fori_loop(0, blocks, gated, jnp.zeros((tokens, BLK), F32))
        stat = jnp.sum(total, axis=1, keepdims=True)
        high = stat.astype(BF16).astype(F32)
        lane = lax.broadcasted_iota(jnp.int32, (tokens, BLK), 1)
        stat = jnp.where(lane < BLK // 2, high, stat - high).astype(BF16)

        def back(d, _):
            owner = lax.rem(r + d, n_row)
            for i in range(per_row):
                block_row = owner * per_row + i
                col_owner = lax.div(block_row, per_col)
                place = lax.rem(block_row, per_col)
                j0, j1 = icol[2 * block_row], icol[2 * block_row + 1]
                rows = pl.ds(pl.multiple_of(place * 3 * BLK, BLK), BLK)
                part = dot_nt(jnp.concatenate([dgb[m, j0], dgb[m, j1]], axis=1), wall[col_owner, rows, :])
                rows = pl.ds(pl.multiple_of((place * 3 + 1) * BLK, BLK), BLK)
                part = part + dot_nt(jnp.concatenate([dub[m, j0], dub[m, j1]], axis=1), wall[col_owner, rows, :])
                rss[m, owner, :, i * BLK : (i + 1) * BLK] = part.astype(BF16)
            rss[m, owner, :, width : width + BLK] = stat

            @pl.when(d < n_row)
            def _():
                sum_copy(m, owner, r, d).start()

            return 0

        lax.fori_loop(1, n_row + 1, back, 0)

    def finish(m):
        tile = pl.ds(pl.multiple_of(m * tokens, tokens), tokens)

        def body(d, total):
            owner = lax.rem(r + d, n_row)
            sum_copy(m, owner, owner, 0).wait_recv()
            return total + rsr[m, owner].astype(F32)

        total = lax.fori_loop(1, n_row, body, rss[m, r].astype(F32))
        stat = jnp.sum(total[:, width:], axis=1, keepdims=True) / (BLK // 2)
        scale = rinv[tile, :][:, 0:1]
        gain = xg[r, both : both + 16, :].astype(F32)[0:1, :]
        value = xg[r, tile, :].astype(F32)
        result = dyg[m, r].astype(F32) + gain * scale * total[:, :width]
        result = result - value * (scale * scale * stat / features)
        gin_ref[m] = result.astype(BF16)

        @pl.when(p > 0)
        def _():
            hop_copy(m, p - 1).start()

    def take_dy(m):
        @pl.when(p < n_pipe - 1)
        def _():
            hop_copy(m, p + 1).wait_recv()
            send_dy(m)

    take_dy(0)

    def chain(m, _):
        front(m)

        @pl.when(m == 0)
        def _():
            take_dy(1)

            def turn(b, _):
                xnt[b] = xn[b].T
                return 0

            lax.fori_loop(0, block_rows, turn, 0)

        @pl.when(jnp.logical_and(m == micro - 1, p == 0))
        def _():
            grads_sibling()

        finish(m)
        return 0

    lax.fori_loop(0, micro, chain, 0)

    @pl.when(p > 0)
    def _():
        grads_sibling()

    def grads_ring(step, _):
        k = lax.rem(step + 2, n_y)
        target = lax.rem(y + k, n_y) * 2 + core
        for which in range(3):
            pair_copy(which, k).wait_recv()

        def emit(which, rows, value):
            value = value + dr[which, k, rows, :].astype(F32)
            own[which, rows, :] = value
            ys[which, k, rows, :] = value.astype(BF16)

        grads(target, emit)

        @pl.when(k > 0)
        def _():
            for which in range(3):
                ring_copy(which, k, target).start()

        return 0

    def ring_order(step, _):
        return grads_ring(jnp.where(step == 0, 0, jnp.where(step == 1, 1, jnp.where(step == 2, 3, 2))), 0)

    lax.fori_loop(0, n_y, ring_order, 0)

    def collect(k, _):
        for which in range(3):
            ring_copy(which, k, sibling).wait_recv()
            own[which] = own[which] + yr[which, k].astype(F32)
        return 0

    lax.fori_loop(1, n_y, collect, 0)
    for i in range(per_col):
        for which, (ref, cnt) in enumerate(((ggate_ref, icnt), (gup_ref, icnt), (gdown_ref, ocnt))):
            live = cnt[c * per_col + i]
            slot = lax.broadcasted_iota(jnp.int32, (BLK, 2 * BLK), 1) // BLK
            rows = slice(i * BLK, (i + 1) * BLK)
            ref[rows, :] = jnp.where(slot < live, own[which, rows, :], 0.0).astype(BF16)

    for number in range(14):
        weights(c, 0, sibling, number).wait_send()

    def sent(d, _):
        other = lax.rem(r + d, n_row)
        x_copy(r, other, d).wait_send()
        for m in range(micro):
            dy_copy(m, r, other, d).wait_send()
            sum_copy(m, other, r, d).wait_send()
        return 0

    lax.fori_loop(1, n_row, sent, 0)

    @pl.when(p > 0)
    def _():
        for m in range(micro):
            hop_copy(m, p - 1).wait_send()

    for which in range(3):
        for k in range(n_y):
            pair_copy(which, k).wait_send()
            if k > 0:
                ring_copy(which, k, sibling).wait_send()


def local(sizes, inputs, grad_out, norm_gain, gate_weight, up_weight, down_weight, inner_cols, inner_counts, outer_cols, outer_counts):
    n_pipe, n_row, n_y, blocks = sizes
    _, micro, tokens, width = inputs.shape
    both = micro * tokens
    block_rows = width * n_row // BLK
    slots = 2 * block_rows
    rows = gate_weight.shape[1]
    icol, ocol = inner_cols.reshape(slots), outer_cols.reshape(slots)
    icnt, ocnt = inner_counts.reshape(block_rows), outer_counts.reshape(block_rows)
    smem = pl.BlockSpec(memory_space=pltpu.SMEM)
    vmem = pl.BlockSpec(memory_space=pltpu.VMEM)
    table = (
        jax.ShapeDtypeStruct((slots,), jnp.int32),
        jax.ShapeDtypeStruct((slots,), F32),
        jax.ShapeDtypeStruct((blocks,), jnp.int32),
        jax.ShapeDtypeStruct((blocks,), F32),
    )
    tables = pl.pallas_call(
        functools.partial(sort_kernel, blocks),
        out_shape=table + table,
        in_specs=[smem, smem],
        out_specs=[smem] * 8,
        scratch_shapes=[pltpu.SMEM((blocks + 1,), jnp.int32)],
        name="order_slots",
    )(icol, ocol)
    dma = pltpu.SemaphoreType.DMA
    weight_out = jax.ShapeDtypeStruct((rows, 2 * BLK), BF16)
    grad_in, gate, up, down = pl.pallas_call(
        functools.partial(main_kernel, sizes),
        out_shape=(jax.ShapeDtypeStruct((micro, tokens, width), BF16), weight_out, weight_out, weight_out),
        in_specs=[vmem] * 6 + [smem] * 12,
        out_specs=[vmem] * 4,
        scratch_shapes=[
            pltpu.VMEM((2 * n_y, 3 * rows, 2 * BLK), BF16),
            pltpu.VMEM((n_row, both + 16, width), BF16),
            pltpu.VMEM((block_rows, both, BLK), BF16),
            pltpu.VMEM((block_rows, BLK, both), BF16),
            pltpu.VMEM((both, BLK), F32),
            pltpu.VMEM((slots, both, BLK), F32),
            pltpu.VMEM((slots, both, BLK), F32),
            pltpu.VMEM((slots, both, BLK), F32),
            pltpu.VMEM((slots, both, BLK), F32),
            pltpu.VMEM((micro, blocks, tokens, BLK), F32),
            pltpu.VMEM((micro, blocks, tokens, BLK), F32),
            pltpu.VMEM((micro, blocks, tokens, BLK), F32),
            pltpu.VMEM((micro, blocks, tokens, BLK), BF16),
            pltpu.VMEM((micro, blocks, tokens, BLK), BF16),
            pltpu.VMEM((micro, blocks, tokens, BLK), BF16),
            pltpu.VMEM((micro, n_row, tokens, width), BF16),
            pltpu.VMEM((micro, n_row, tokens, width + BLK), BF16),
            pltpu.VMEM((micro, n_row, tokens, width + BLK), BF16),
            pltpu.VMEM((3, n_y, rows, 2 * BLK), BF16),
            pltpu.VMEM((3, n_y, rows, 2 * BLK), BF16),
            pltpu.VMEM((3, n_y, rows, 2 * BLK), BF16),
            pltpu.VMEM((3, n_y, rows, 2 * BLK), BF16),
            pltpu.VMEM((3, rows, 2 * BLK), F32),
            dma((14,)), dma((2 * n_y, 2)),
            dma((n_row,)), dma((n_row,)),
            dma((micro, n_row)), dma((micro, n_row)),
            dma((micro,)), dma((micro,)),
            dma((micro, n_row)), dma((micro, n_row)),
            dma((3, n_y)), dma((3, n_y)),
            dma((3, n_y)), dma((3, n_y)),
        ],
        compiler_params=pltpu.CompilerParams(collective_id=0, has_side_effects=True, vmem_limit_bytes=56 * 1024 * 1024),
        name="backward",
    )(
        inputs.reshape(both, width), grad_out, norm_gain,
        gate_weight.reshape(rows, 2 * BLK), up_weight.reshape(rows, 2 * BLK), down_weight.reshape(rows, 2 * BLK),
        icol, icnt, ocol, ocnt, *tables,
    )
    return grad_in[None], gate[None], up[None], down[None]


def solution(mesh):
    in_specs = (
        P("pipe", None, "col", "row"),
        P(None, "col", "row"),
        P("pipe", "row"),
        P("pipe", "col", "row"),
        P("pipe", "col", "row"),
        P("pipe", "col", "row"),
        P("pipe", None, "row"),
        P("pipe", None, "row"),
        P("pipe", None, "row"),
        P("pipe", None, "row"),
    )
    out_specs = (
        P("pipe", None, "col", "row"),
        P("pipe", "col", "row"),
        P("pipe", "col", "row"),
        P("pipe", "col", "row"),
    )
    sizes = (mesh.shape["pipe"], mesh.shape["row"], mesh.shape["col"] // 2, FF // (mesh.shape["row"] * BLK))
    return jax.shard_map(functools.partial(local, sizes), mesh=mesh, in_specs=in_specs, out_specs=out_specs, check_vma=False)
```

```python
import functools

import jax
import jax.numpy as jnp
from jax import lax
from jax.experimental import pallas as pl
from jax.experimental.pallas import tpu as pltpu
from jax.sharding import PartitionSpec as P

FF = 14336
BLK = 128
EPSILON = 1e-05
MESH = pl.DeviceIdType.MESH
F32 = jnp.float32
BF16 = jnp.bfloat16


CHUNKS = 4
FACTOR_SECTIONS = 2


def dot(a, b):
    return jnp.dot(a, b, preferred_element_type=F32)


def pick(index, values):
    result = values[-1]
    for i in reversed(range(len(values) - 1)):
        result = jnp.where(index == i, values[i], result)
    return result


def slot_table(col):
    block_rows = col.shape[1]
    square = (block_rows, block_rows)
    eye = lax.broadcasted_iota(jnp.int32, square, 0) == lax.broadcasted_iota(jnp.int32, square, 1)
    lane = lax.broadcasted_iota(jnp.int32, (1, block_rows), 1)
    down = lax.broadcasted_iota(jnp.int32, (block_rows, BLK), 0)
    place = lax.broadcasted_iota(jnp.int32, (block_rows, BLK), 1)

    def upright(row):
        return jnp.sum(jnp.where(eye, jnp.broadcast_to(row, square), 0), axis=1, keepdims=True)

    rows = [col[s : s + 1, :] for s in range(2)]
    keys = [rows[s] * (2 * block_rows) + s * block_rows + lane for s in range(2)]
    order, keep, upto, count = 0, 0, 0, 0
    for s in range(2):
        key, block = upright(keys[s]), upright(rows[s])
        rank = sum(jnp.sum(jnp.where(keys[t] < key, 1, 0), axis=1, keepdims=True) for t in range(2))
        first = sum(jnp.sum(jnp.where(rows[t] < block, 1, 0), axis=1, keepdims=True) for t in range(2))
        here = rank == place
        order = order + jnp.sum(jnp.where(here, down + s * block_rows, 0), axis=0, keepdims=True)
        keep = keep + jnp.sum(jnp.where(here, jnp.where(rank != first, 1, 0), 0), axis=0, keepdims=True)
        upto = upto + jnp.sum(jnp.where(block <= place, 1, 0), axis=0, keepdims=True)
        count = count + jnp.sum(jnp.where(block == place, 1, 0), axis=0, keepdims=True)
    return order, keep, jnp.maximum(upto - 1, 0), jnp.minimum(count, 1)


def main_kernel(
    sizes,
    x_ref, go_ref, gain_ref, gate_ref, up_ref, down_ref, icol_rows, ocol_rows,
    icol, icnt, ocol, ocnt,
    gin_ref, ggate_ref, gup_ref, gdown_ref,
    wall, wt, xg, xn, rinv, pg, pu, sg, ab, bb, cb, hb, pool, dhall, dgb, dub, dyg, dyr, xnr, rss, rsr, dgl, dul, hl, acc, tabv, tab,
    tabsem, wsend, wrecv, xsend, xrecv, gsend, grecv, hsend, hrecv, rsend, rrecv,
    asend, arecv, nsend, nrecv, dsend, drecv, csend, crecv, psend, precv, ysend, yrecv,
):
    n_pipe, n_row, n_y, blocks = sizes
    n_col, n_x = 2 * n_y, n_row // 2
    both, width = x_ref.shape
    tokens = both // CHUNKS
    features = width * n_row
    block_rows = features // BLK
    per = block_rows // n_row
    slots = 2 * block_rows
    piece = 3 * BLK
    span = 3 * blocks * both
    block = 2 * per * BLK

    p = lax.axis_index("pipe")
    r = lax.axis_index("row")
    c = lax.axis_index("col")
    y = lax.div(c, 2)
    core = lax.rem(c, 2)
    x = lax.rem(r, n_x)
    by_factors = p <= FACTOR_SECTIONS - 1
    partner = lax.rem(r + n_x, n_row)

    def place(row):
        return lax.rem(row, n_x) * 2 + lax.div(row, n_x)

    def column(dy, dcore):
        return lax.rem(y + dy, n_y) * 2 + lax.rem(core + dcore, 2)

    up_y, down_y, sibling = column(1, 0), column(n_y - 1, 0), column(0, 1)

    barrier = pltpu.get_barrier_semaphore()

    def greet(d, _):
        pl.semaphore_signal(barrier, inc=1, device_id={"row": lax.rem(r + d, n_row)}, device_id_type=MESH)
        pl.semaphore_signal(barrier, inc=1, device_id={"col": lax.rem(c + d, n_col)}, device_id_type=MESH)
        return 0

    lax.fori_loop(1, n_row, greet, 0)

    @pl.when(p > 0)
    def _():
        for row in (r, partner):
            pl.semaphore_signal(barrier, inc=1, device_id={"pipe": p - 1, "row": row}, device_id_type=MESH)

    @pl.when(p < n_pipe - 1)
    def _():
        for row in (r, partner):
            pl.semaphore_signal(barrier, inc=1, device_id={"pipe": p + 1, "row": row}, device_id_type=MESH)

    xg[r, 0:both, :] = x_ref[...]
    xg[r, both : both + 16, :] = jnp.broadcast_to(gain_ref[...].astype(F32), (16, width)).astype(BF16)
    for i in range(per):
        for which, (ref, cnt) in enumerate(((gate_ref, icnt), (up_ref, icnt), (down_ref, ocnt))):
            live = cnt[c * per + i]
            slot = lax.broadcasted_iota(jnp.int32, (BLK, 2 * BLK), 1) // BLK
            value = ref[i * BLK : (i + 1) * BLK, :].astype(F32)
            wall[c, (i * 3 + which) * BLK : (i * 3 + which + 1) * BLK, :] = jnp.where(slot < live, value, 0.0).astype(BF16)

    @pl.when(p == n_pipe - 1)
    def _():
        for k in range(CHUNKS):
            dyg[k, place(r)] = go_ref[k * tokens : (k + 1) * tokens, :]

    pl.semaphore_wait(barrier, n_row - 1 + n_col - 1 + jnp.where(p > 0, 2, 0) + jnp.where(p < n_pipe - 1, 2, 0))

    def remote(src, dst, send, recv, target):
        return pltpu.make_async_remote_copy(src_ref=src, dst_ref=dst, send_sem=send, recv_sem=recv, device_id=target, device_id_type=MESH)

    def weights(owner, q, target, number):
        share = wall.at[owner, pl.ds(pl.multiple_of(q * piece, piece), piece), :]
        return remote(share, share, wsend.at[number], wrecv.at[owner, q], {"col": target})

    def x_copy(owner, target, number):
        return remote(xg.at[owner], xg.at[owner], xsend.at[number], xrecv.at[owner], {"row": target})

    def dy_copy(k, source, target, number):
        pair = dyg.at[k, pl.ds(source * 2, 2)]
        row = lax.div(r, n_x) * n_x + target
        return remote(pair, pair, gsend.at[k, number], grecv.at[k, source], {"row": row})

    def hop_copy(k, pipe, row, number):
        rows = pl.ds(pl.multiple_of(k * tokens, tokens), tokens)
        return remote(gin_ref.at[rows, :], dyg.at[k, place(r)], hsend.at[k, number], hrecv.at[k, number], {"pipe": pipe, "row": row})

    def swap_copy(k):
        share = dyg.at[k, place(r)]
        return remote(share, share, hsend.at[k, 1], hrecv.at[k, 1], {"row": partner})

    def sum_copy(k, target, source, number):
        return remote(rss.at[k, target], rsr.at[k, source], rsend.at[k, number], rrecv.at[k, source], {"row": target})

    def factor_copy(owner, target, number):
        share = pool.at[pl.ds(pl.multiple_of(owner * span, span), span), :]
        return remote(share, share, asend.at[number], arecv.at[owner], {"col": target})

    def share_start(part, which, k):
        if part < 2:
            return ((part * 3 + which) * n_y + k) * block
        return (6 * n_y + ((part - 2) * 3 + which) * (n_y - 1) + k - 1) * block

    def shares(part, which, k):
        return pl.ds(pl.multiple_of(share_start(part, which, k), block), block)

    def pair_copy(which, k):
        return remote(pool.at[shares(0, which, k), :], pool.at[shares(1, which, k), :], psend.at[which, k], precv.at[which, k], {"col": sibling})

    def ring_copy(which, k, target):
        return remote(pool.at[shares(2, which, k), :], pool.at[shares(3, which, k), :], ysend.at[which, k], yrecv.at[which, k], {"col": target})

    def dh_copy(k, owner, target, number):
        return remote(dhall.at[k, owner], dhall.at[k, owner], dsend.at[k, number], drecv.at[k, owner], {"col": target})

    def xn_copy(target, source, number):
        return remote(xn.at[pl.ds(target * per, per)], xnr.at[source], nsend.at[number], nrecv.at[source], {"col": target})

    def dyc_copy(k, target, source, number):
        return remote(dyg.at[k, place(target)], dyr.at[k, source], csend.at[k, number], crecv.at[k, source], {"col": target})

    def send_dy(k):
        def body(d, _):
            dy_copy(k, x, lax.rem(x + d, n_x), d).start()
            return 0

        lax.fori_loop(1, n_x, body, 0)

    def send_x(d, _):
        x_copy(r, lax.rem(r + d, n_row), d).start()
        return 0

    for q in range(per):
        weights(c, q, up_y, q).start()
        weights(c, (q + 2) % per, down_y, per + q).start()
    lax.fori_loop(1, n_row, send_x, 0)
    for q in range(per):
        weights(c, q, sibling, 8 + q).start()

    @pl.when(p == n_pipe - 1)
    def _():
        def body(k, _):
            swap_copy(k).start()
            return 0

        lax.fori_loop(0, CHUNKS, body, 0)

    for at, ref in ((0, icol_rows), (4, ocol_rows)):
        for row, value in enumerate(slot_table(ref[...])):
            tabv[at + row : at + row + 1, :] = value
    table = pltpu.make_async_copy(tabv, tab, tabsem)
    table.start()
    acc[...] = jnp.zeros_like(acc)
    table.wait()

    rinv[...] = jnp.zeros_like(rinv)

    def squares(d, _):
        owner = lax.rem(r + d, n_row)

        @pl.when(d > 0)
        def _():
            x_copy(owner, owner, 0).wait_recv()

        total = rinv[...]
        for i in range(per):
            value = xg[owner, 0:both, i * BLK : (i + 1) * BLK].astype(F32)
            total = total + value * value
        rinv[...] = total
        return 0

    lax.fori_loop(0, n_row, squares, 0)
    mean = jnp.sum(rinv[...], axis=1, keepdims=True) / features
    rinv[...] = jnp.broadcast_to(lax.rsqrt(mean + EPSILON), (both, BLK))

    def norm(owner, _):
        scale = rinv[...]
        for i in range(per):
            lanes = slice(i * BLK, (i + 1) * BLK)
            gain = xg[owner, both : both + 16, lanes].astype(F32)[0:1, :]
            value = xg[owner, 0:both, lanes].astype(F32)
            xn[owner * per + i] = (value * scale * gain).astype(BF16)
        return 0

    lax.fori_loop(0, n_row, norm, 0)

    def first_dy(k, _):
        swap_copy(k).wait_recv()
        send_dy(k)
        return 0

    @pl.when(p == n_pipe - 1)
    def _():
        lax.fori_loop(0, CHUNKS, first_dy, 0)

    def use(owner, q):
        block_row = owner * per + q
        value = xn[block_row]
        for which, out in ((0, pg), (1, pu)):
            rows = pl.ds(pl.multiple_of(q * piece + which * BLK, BLK), BLK)
            weight = wall[owner, rows, :]
            product = dot(value, weight)
            out[block_row] = product[:, :BLK]
            out[block_rows + block_row] = product[:, BLK:]
            wt[block_row, which * 2 * BLK : (which + 1) * 2 * BLK, :] = weight.T

    turns = (0, 0, 0, 0, n_y - 1, 1, n_y - 1, 1, n_y - 1, 1, n_y - 1, 1, 2, 2, 2, 2)
    quarters = (0, 1, 2, 3, 0, 2, 1, 3, 2, 0, 3, 1, 0, 2, 1, 3)
    steps = len(turns)

    def arrive(s, _):
        @pl.when(s < steps)
        def _():
            q = pick(s, quarters)
            owner = column(pick(s, turns), 0)

            @pl.when(s >= 4)
            def _():
                weights(owner, q, sibling, 0).wait_recv()

                @pl.when(s < 8)
                def _():
                    target = jnp.where(lax.rem(s, 2) == 0, up_y, down_y)
                    weights(owner, q, target, 8 + s).start()

                weights(owner, q, sibling, 12 + s).start()

            use(owner, q)

        @pl.when(s >= 2)
        def _():
            q = pick(s - 2, quarters)
            owner = column(pick(s - 2, turns), 1)
            weights(owner, q, sibling, 0).wait_recv()
            use(owner, q)

        return 0

    lax.fori_loop(0, steps + 2, arrive, 0)

    def add_slots(at, source, rows):
        def body(i, total):
            total = total * tab[at + 1, i].astype(F32) + source[tab[at, i], 0:rows, :]
            sg[i, 0:rows, :] = total
            return total

        lax.fori_loop(0, slots, body, jnp.zeros((rows, BLK), F32), unroll=4)

    add_slots(0, pg, both)

    def gates(j, _):
        ab[j] = sg[tab[2, j]] * tab[3, j].astype(F32)
        return 0

    lax.fori_loop(0, blocks, gates, 0)
    add_slots(0, pu, both)

    def hidden(j, _):
        g = ab[j]
        u = sg[tab[2, j]] * tab[3, j].astype(F32)
        s = jax.nn.sigmoid(g)
        a = u * s * (1.0 + g * (1.0 - s))
        b = g * s
        ab[j] = a
        bb[j] = b
        cb[j] = a * g + b * u
        h = (b * u).astype(BF16)
        hb[j] = h

        @pl.when(by_factors)
        def _():
            for which, value in enumerate((a.astype(BF16), b.astype(BF16), h)):
                pool[pl.ds(pl.multiple_of(c * span + (which * blocks + j) * both, both), both), :] = value

        return 0

    lax.fori_loop(0, blocks, hidden, 0)

    def send_xn(d, _):
        xn_copy(lax.rem(c + d, n_col), c, d).start()
        return 0

    def send_factors():
        for d in range(1, n_y):
            factor_copy(c, column(d, 0), d - 1).start()
        factor_copy(c, sibling, n_y - 1).start()

    def products(k):
        def body(d, _):
            from_x = lax.rem(x + d, n_x)

            @pl.when(d > 0)
            def _():
                dy_copy(k, from_x, from_x, 0).wait_recv()

            for z in range(2):
                owner = z * n_x + from_x
                for i in range(per):
                    block_row = owner * per + i
                    product = dot(dyg[k, from_x * 2 + z, :, i * BLK : (i + 1) * BLK], wall[owner, (i * 3 + 2) * BLK : (i * 3 + 3) * BLK, :])
                    pg[block_row, 0:tokens, :] = product[:, :BLK]
                    pg[block_rows + block_row, 0:tokens, :] = product[:, BLK:]
            return 0

        lax.fori_loop(0, n_x, body, 0)

    def back(k):
        mine = pl.ds(pl.multiple_of(k * tokens, tokens), tokens)
        add_slots(4, pg, tokens)

        def gated(j, total):
            dh = sg[tab[6, j], 0:tokens, :] * tab[7, j].astype(F32)
            dgb[j, mine, :] = (dh * ab[j, mine, :]).astype(BF16)
            dub[j, mine, :] = (dh * bb[j, mine, :]).astype(BF16)
            dhall[k, c, j] = dh.astype(BF16)
            return total + dh * cb[j, mine, :]

        total = lax.fori_loop(0, blocks, gated, jnp.zeros((tokens, BLK), F32))

        @pl.when(by_factors)
        def _():
            for d in range(1, n_y):
                dh_copy(k, c, column(d, 0), d - 1).start()
            dh_copy(k, c, sibling, n_y - 1).start()

        stat = jnp.sum(total, axis=1, keepdims=True)
        high = stat.astype(BF16).astype(F32)
        lane = lax.broadcasted_iota(jnp.int32, (tokens, BLK), 1)
        stat = jnp.where(lane < BLK // 2, high, stat - high).astype(BF16)

        def body(d, _):
            owner = lax.rem(r + d, n_row)
            for i in range(per):
                block_row = owner * per + i
                j0, j1 = icol[0, block_row], icol[1, block_row]
                left = jnp.concatenate([dgb[j0, mine, :], dgb[j1, mine, :], dub[j0, mine, :], dub[j1, mine, :]], axis=1)
                rss[k, owner, :, i * BLK : (i + 1) * BLK] = dot(left, wt[block_row]).astype(BF16)
            rss[k, owner, :, width : width + BLK] = stat

            @pl.when(d < n_row)
            def _():
                sum_copy(k, owner, r, d).start()

            return 0

        lax.fori_loop(1, n_row + 1, body, 0)

        @pl.when(by_factors)
        def _():
            dyr[k, c] = dyg[k, place(c)]

            def send(d, _):
                dyc_copy(k, lax.rem(c + d, n_col), c, d).start()
                return 0

            lax.fori_loop(1, n_col, send, 0)

    def finish(k):
        mine = pl.ds(pl.multiple_of(k * tokens, tokens), tokens)

        def body(d, total):
            owner = lax.rem(r + d, n_row)
            sum_copy(k, owner, owner, 0).wait_recv()
            return total + rsr[k, owner].astype(F32)

        total = lax.fori_loop(1, n_row, body, rss[k, r].astype(F32))
        stat = jnp.sum(total[:, width:], axis=1, keepdims=True) / (BLK // 2)
        scale = rinv[mine, :][:, 0:1]
        gain = xg[r, both : both + 16, :].astype(F32)[0:1, :]
        value = xg[r, mine, :].astype(F32)
        result = dyg[k, place(r)].astype(F32) + gain * scale * total[:, :width]
        result = result - value * (scale * scale * stat / features)
        gin_ref[mine, :] = result.astype(BF16)

        @pl.when(p > 0)
        def _():
            hop_copy(k, p - 1, r, 0).start()
            hop_copy(k, p - 1, partner, 1).start()

    def take_dy(k):
        @pl.when(p < n_pipe - 1)
        def _():
            hop_copy(k, p + 1, r, 0).wait_recv()
            hop_copy(k, p + 1, partner, 1).wait_recv()
            send_dy(k)

    def pass_on(k):
        for d in range(1, n_y):
            owner = column(d, 0)

            @pl.when(k == 0)
            def _(owner=owner, d=d):
                factor_copy(owner, owner, 0).wait_recv()
                factor_copy(owner, sibling, n_y - 1 + d).start()

            dh_copy(k, owner, owner, 0).wait_recv()
            dh_copy(k, owner, sibling, n_y - 1 + d).start()

    def down_part(k):
        @pl.when(k == 0)
        def _():
            def body(d, _):
                other = lax.rem(c + d, n_col)
                xn_copy(other, other, 0).wait_recv()
                return 0

            lax.fori_loop(1, n_col, body, 0)

        def body(d, _):
            other = lax.rem(c + d, n_col)
            dyc_copy(k, other, other, 0).wait_recv()
            return 0

        lax.fori_loop(1, n_col, body, 0)

    def grads(k):
        mine = pl.ds(pl.multiple_of(k * tokens, tokens), tokens)
        for d in range(n_y):
            owner = column(d, 1)

            @pl.when(k == 0)
            def _(owner=owner):
                factor_copy(owner, sibling, 0).wait_recv()

            dh_copy(k, owner, sibling, 0).wait_recv()

        def body(j, _):
            for o in range(n_col):
                rows = slice(o * tokens, (o + 1) * tokens)
                dh = dhall[k, o, j].astype(F32)
                a, b, h = (
                    pool[pl.ds(pl.multiple_of(o * span + (which * blocks + j) * both + k * tokens, tokens), tokens), :] for which in range(3)
                )
                dgl[j, rows, :] = (dh * a.astype(F32)).astype(BF16)
                dul[j, rows, :] = (dh * b.astype(F32)).astype(BF16)
                hl[j, rows, :] = h
            return 0

        lax.fori_loop(0, blocks, body, 0)
        for i in range(per):
            block_row = c * per + i
            j0, j1 = icol[0, block_row], icol[1, block_row]
            q0, q1 = ocol[0, block_row], ocol[1, block_row]
            left = jnp.concatenate([xnr[o, i, mine, :] for o in range(n_col)], axis=0).T
            acc[0, i] = acc[0, i] + dot(left, jnp.concatenate([dgl[j0], dgl[j1]], axis=1))
            acc[1, i] = acc[1, i] + dot(left, jnp.concatenate([dul[j0], dul[j1]], axis=1))
            left = jnp.concatenate([dyr[k, o, :, i * BLK : (i + 1) * BLK] for o in range(n_col)], axis=0).T
            acc[2, i] = acc[2, i] + dot(left, jnp.concatenate([hl[q0], hl[q1]], axis=1))

    def own_grads(owner, emit):
        for i in range(per):
            block_row = owner * per + i
            j0, j1 = icol[0, block_row], icol[1, block_row]
            q0, q1 = ocol[0, block_row], ocol[1, block_row]
            left = xn[block_row].T
            emit(0, i, dot(left, jnp.concatenate([dgb[j0], dgb[j1]], axis=1)))
            emit(1, i, dot(left, jnp.concatenate([dub[j0], dub[j1]], axis=1)))
            dy = jnp.concatenate([dyg[k, place(owner), :, i * BLK : (i + 1) * BLK] for k in range(CHUNKS)], axis=0)
            emit(2, i, dot(dy.T, jnp.concatenate([hb[q0], hb[q1]], axis=1)))

    def part_rows(part, which, k, i, s):
        start = share_start(part, which, k) + (i * 2 + s) * BLK
        return pl.ds(pl.multiple_of(start, BLK), BLK)

    def put(part, which, k, i, value):
        for s in range(2):
            pool[part_rows(part, which, k, i, s), :] = value[:, s * BLK : (s + 1) * BLK].astype(BF16)

    def get(part, which, k, i):
        return jnp.concatenate([pool[part_rows(part, which, k, i, s), :] for s in range(2)], axis=1).astype(F32)

    def to_sibling(k, _):
        own_grads(lax.rem(y + k, n_y) * 2 + (1 - core), lambda which, i, value: put(0, which, k, i, value))
        for which in range(3):
            pair_copy(which, k).start()
        return 0

    def to_ring(step, _):
        k = pick(step, (2, 1, 3, 0))
        target = lax.rem(y + k, n_y) * 2 + core
        for which in range(3):
            pair_copy(which, k).wait_recv()

        def emit(which, i, value):
            value = value + get(1, which, k, i)
            acc[which, i] = value

            @pl.when(k > 0)
            def _():
                put(2, which, k, i, value)

        own_grads(target, emit)

        @pl.when(k > 0)
        def _():
            for which in range(3):
                ring_copy(which, k, target).start()

        return 0

    def collect(k, _):
        for which in range(3):
            ring_copy(which, k, sibling).wait_recv()
            for i in range(per):
                acc[which, i] = acc[which, i] + get(3, which, k, i)
        return 0

    @pl.when(by_factors)
    def _():
        xnr[c] = xn[pl.ds(c * per, per)]
        send_factors()
        lax.fori_loop(1, n_col, send_xn, 0)

    take_dy(0)

    def step(s, _):
        @pl.when(s < CHUNKS)
        def _():
            products(s)

            @pl.when(s < CHUNKS - 1)
            def _():
                take_dy(s + 1)

            back(s)

        @pl.when(jnp.logical_and(s >= lead + 1, s < lead + 1 + CHUNKS))
        def _():
            grads(s - lead - 1)

        @pl.when(jnp.logical_and(s >= lead, s < lead + CHUNKS))
        def _():
            down_part(s - lead)
            pass_on(s - lead)

        @pl.when(jnp.logical_and(s >= 1, s < CHUNKS + 1))
        def _():
            finish(s - 1)

        return 0

    lead = jnp.where(p == 0, 1, jnp.where(by_factors, CHUNKS + 1, 3 * CHUNKS))
    lax.fori_loop(0, 2 * CHUNKS + 2, step, 0)

    @pl.when(jnp.logical_not(by_factors))
    def _():
        lax.fori_loop(0, n_y, to_sibling, 0)
        lax.fori_loop(0, n_y, to_ring, 0)
        lax.fori_loop(1, n_y, collect, 0)

    for i in range(per):
        for which, (ref, cnt) in enumerate(((ggate_ref, icnt), (gup_ref, icnt), (gdown_ref, ocnt))):
            live = cnt[c * per + i]
            slot = lax.broadcasted_iota(jnp.int32, (BLK, 2 * BLK), 1) // BLK
            ref[i * BLK : (i + 1) * BLK, :] = jnp.where(slot < live, acc[which, i], 0.0).astype(BF16)

    def sent_weights(number, _):
        weights(c, 0, sibling, number).wait_send()
        return 0

    lax.fori_loop(0, 28, sent_weights, 0)

    def sent(d, _):
        other = lax.rem(r + d, n_row)
        x_copy(r, other, d).wait_send()
        for k in range(CHUNKS):
            sum_copy(k, other, r, d).wait_send()
        return 0

    lax.fori_loop(1, n_row, sent, 0)

    def sent_dy(d, _):
        for k in range(CHUNKS):
            dy_copy(k, x, lax.rem(x + d, n_x), d).wait_send()
        return 0

    lax.fori_loop(1, n_x, sent_dy, 0)

    @pl.when(p == n_pipe - 1)
    def _():
        for k in range(CHUNKS):
            swap_copy(k).wait_send()

    @pl.when(p > 0)
    def _():
        for k in range(CHUNKS):
            hop_copy(k, p - 1, r, 0).wait_send()
            hop_copy(k, p - 1, partner, 1).wait_send()

    @pl.when(jnp.logical_not(by_factors))
    def _():
        for which in range(3):
            for k in range(n_y):
                pair_copy(which, k).wait_send()
                if k > 0:
                    ring_copy(which, k, sibling).wait_send()

    @pl.when(by_factors)
    def _():
        def sent_beside(d, _):
            beside = lax.rem(c + d, n_col)
            xn_copy(beside, c, d).wait_send()
            for k in range(CHUNKS):
                dyc_copy(k, beside, c, d).wait_send()
            return 0

        lax.fori_loop(1, n_col, sent_beside, 0)

        def sent_factors(number, _):
            factor_copy(c, sibling, number).wait_send()
            for k in range(CHUNKS):
                dh_copy(k, c, sibling, number).wait_send()
            return 0

        lax.fori_loop(0, 2 * n_y - 1, sent_factors, 0)


def hand_over(a, b, c, d, out_a, out_b, out_c, out_d):
    for src, dst in ((a, out_a), (b, out_b), (c, out_c), (d, out_d)):
        dst[...] = src[...]


def local(sizes, inputs, grad_out, norm_gain, gate_weight, up_weight, down_weight, inner_cols, inner_counts, outer_cols, outer_counts):
    n_pipe, n_row, n_y, blocks = sizes
    n_col, n_x = 2 * n_y, n_row // 2
    _, micro, tokens, width = inputs.shape
    both = micro * tokens
    small = both // CHUNKS
    block_rows = width * n_row // BLK
    per = block_rows // n_row
    slots = 2 * block_rows
    rows = gate_weight.shape[1]
    icol, ocol = inner_cols[0].T, outer_cols[0].T
    icnt, ocnt = inner_counts.reshape(block_rows), outer_counts.reshape(block_rows)
    smem = pl.BlockSpec(memory_space=pltpu.SMEM)
    vmem = pl.BlockSpec(memory_space=pltpu.VMEM)
    dma = pltpu.SemaphoreType.DMA
    weight_out = jax.ShapeDtypeStruct((rows, 2 * BLK), BF16)
    outs = (jax.ShapeDtypeStruct((both, width), BF16), weight_out, weight_out, weight_out)
    results = pl.pallas_call(
        functools.partial(main_kernel, sizes),
        out_shape=outs,
        in_specs=[vmem] * 8 + [smem] * 4,
        out_specs=[vmem] * 4,
        scratch_shapes=[
            pltpu.VMEM((n_col, 3 * rows, 2 * BLK), BF16),
            pltpu.VMEM((block_rows, 4 * BLK, BLK), BF16),
            pltpu.VMEM((n_row, both + 16, width), BF16),
            pltpu.VMEM((block_rows, both, BLK), BF16),
            pltpu.VMEM((both, BLK), F32),
            pltpu.VMEM((slots, both, BLK), F32),
            pltpu.VMEM((slots, both, BLK), F32),
            pltpu.VMEM((slots, both, BLK), F32),
            pltpu.VMEM((blocks, both, BLK), F32),
            pltpu.VMEM((blocks, both, BLK), F32),
            pltpu.VMEM((blocks, both, BLK), F32),
            pltpu.VMEM((blocks, both, BLK), BF16),
            pltpu.VMEM((max(n_col * 3 * blocks * both, (12 * n_y - 6) * 2 * rows), BLK), BF16),
            pltpu.VMEM((CHUNKS, n_col, blocks, small, BLK), BF16),
            pltpu.VMEM((blocks, both, BLK), BF16),
            pltpu.VMEM((blocks, both, BLK), BF16),
            pltpu.VMEM((CHUNKS, n_row, small, width), BF16),
            pltpu.VMEM((CHUNKS, n_col, small, width), BF16),
            pltpu.VMEM((n_col, per, both, BLK), BF16),
            pltpu.VMEM((CHUNKS, n_row, small, width + BLK), BF16),
            pltpu.VMEM((CHUNKS, n_row, small, width + BLK), BF16),
            pltpu.VMEM((blocks, n_col * small, BLK), BF16),
            pltpu.VMEM((blocks, n_col * small, BLK), BF16),
            pltpu.VMEM((blocks, n_col * small, BLK), BF16),
            pltpu.VMEM((3, per, BLK, 2 * BLK), F32),
            pltpu.VMEM((8, BLK), jnp.int32),
            pltpu.SMEM((8, BLK), jnp.int32),
            dma,
            dma((28,)), dma((n_col, per)),
            dma((n_row,)), dma((n_row,)),
            dma((CHUNKS, n_x)), dma((CHUNKS, n_x)),
            dma((CHUNKS, 2)), dma((CHUNKS, 2)),
            dma((CHUNKS, n_row)), dma((CHUNKS, n_row)),
            dma((2 * n_y - 1,)), dma((n_col,)),
            dma((n_col,)), dma((n_col,)),
            dma((CHUNKS, 2 * n_y - 1)), dma((CHUNKS, n_col)),
            dma((CHUNKS, n_col)), dma((CHUNKS, n_col)),
            dma((3, n_y)), dma((3, n_y)),
            dma((3, n_y)), dma((3, n_y)),
        ],
        compiler_params=pltpu.CompilerParams(collective_id=0, has_side_effects=True, vmem_limit_bytes=60 * 1024 * 1024),
        name="backward",
    )(
        inputs.reshape(both, width), grad_out.reshape(both, width), norm_gain,
        gate_weight.reshape(rows, 2 * BLK), up_weight.reshape(rows, 2 * BLK), down_weight.reshape(rows, 2 * BLK),
        icol, ocol, icol, icnt, ocol, ocnt,
    )
    grad_in, gate, up, down = pl.pallas_call(
        hand_over,
        out_shape=outs,
        in_specs=[vmem] * 4,
        out_specs=[vmem] * 4,
        name="hand_over",
    )(*results)
    return grad_in.reshape(inputs.shape), gate[None], up[None], down[None]


def solution(mesh):
    in_specs = (
        P("pipe", None, "col", "row"),
        P(None, "col", "row"),
        P("pipe", "row"),
        P("pipe", "col", "row"),
        P("pipe", "col", "row"),
        P("pipe", "col", "row"),
        P("pipe", None, "row"),
        P("pipe", None, "row"),
        P("pipe", None, "row"),
        P("pipe", None, "row"),
    )
    out_specs = (
        P("pipe", None, "col", "row"),
        P("pipe", "col", "row"),
        P("pipe", "col", "row"),
        P("pipe", "col", "row"),
    )
    sizes = (mesh.shape["pipe"], mesh.shape["row"], mesh.shape["col"] // 2, FF // (mesh.shape["row"] * BLK))
    return jax.shard_map(functools.partial(local, sizes), mesh=mesh, in_specs=in_specs, out_specs=out_specs, check_vma=False)
```

```python
import functools

import jax
import jax.numpy as jnp
from jax import lax
from jax.experimental import pallas as pl
from jax.experimental.pallas import tpu as pltpu
from jax.sharding import PartitionSpec as P

FF = 14336
BLK = 128
EPSILON = 1e-05
MESH = pl.DeviceIdType.MESH
F32 = jnp.float32
BF16 = jnp.bfloat16


CHUNKS = 8
FACTOR_SECTIONS = 2
AHEAD = 1
LATE = 1
FACTORS_LATE = 2


def dot(a, b):
    return jnp.dot(a, b, preferred_element_type=F32)


def pick(index, values):
    result = values[-1]
    for i in reversed(range(len(values) - 1)):
        result = jnp.where(index == i, values[i], result)
    return result


def slot_table(col):
    block_rows = col.shape[1]
    square = (block_rows, block_rows)
    eye = lax.broadcasted_iota(jnp.int32, square, 0) == lax.broadcasted_iota(jnp.int32, square, 1)
    lane = lax.broadcasted_iota(jnp.int32, (1, block_rows), 1)
    down = lax.broadcasted_iota(jnp.int32, (block_rows, BLK), 0)
    place = lax.broadcasted_iota(jnp.int32, (block_rows, BLK), 1)

    def upright(row):
        return jnp.sum(jnp.where(eye, jnp.broadcast_to(row, square), 0), axis=1, keepdims=True)

    rows = [col[s : s + 1, :] for s in range(2)]
    keys = [rows[s] * (2 * block_rows) + s * block_rows + lane for s in range(2)]
    order, keep, upto, count = 0, 0, 0, 0
    for s in range(2):
        key, block = upright(keys[s]), upright(rows[s])
        rank = sum(jnp.sum(jnp.where(keys[t] < key, 1, 0), axis=1, keepdims=True) for t in range(2))
        first = sum(jnp.sum(jnp.where(rows[t] < block, 1, 0), axis=1, keepdims=True) for t in range(2))
        here = rank == place
        order = order + jnp.sum(jnp.where(here, down + s * block_rows, 0), axis=0, keepdims=True)
        keep = keep + jnp.sum(jnp.where(here, jnp.where(rank != first, 1, 0), 0), axis=0, keepdims=True)
        upto = upto + jnp.sum(jnp.where(block <= place, 1, 0), axis=0, keepdims=True)
        count = count + jnp.sum(jnp.where(block == place, 1, 0), axis=0, keepdims=True)
    return order, keep, jnp.maximum(upto - 1, 0), jnp.minimum(count, 1)


def main_kernel(
    sizes,
    x_ref, go_ref, gain_ref, gate_ref, up_ref, down_ref, icol_rows, ocol_rows,
    icol, icnt, ocol, ocnt,
    gin_ref, ggate_ref, gup_ref, gdown_ref,
    wall, wt, xg, xn, rinv, pg, pu, sg, ab, bb, cb, hb, pool, dhall, dgb, dub, dyg, dyr, xnr, rss, rsr, al, bl, hl, dgl, dul, xnt, acc, tabv, tab,
    tabsem, wsend, wrecv, xsend, xrecv, gsend, grecv, hsend, hrecv, rsend, rrecv,
    asend, arecv, nsend, nrecv, dsend, drecv, csend, crecv, psend, precv, ysend, yrecv,
):
    n_pipe, n_row, n_y, blocks = sizes
    n_col, n_x = 2 * n_y, n_row // 2
    both, width = x_ref.shape
    tokens = both // CHUNKS
    features = width * n_row
    block_rows = features // BLK
    per = block_rows // n_row
    slots = 2 * block_rows
    piece = 3 * BLK
    span = 2 * blocks * both
    block = 2 * per * BLK

    p = lax.axis_index("pipe")
    r = lax.axis_index("row")
    c = lax.axis_index("col")
    y = lax.div(c, 2)
    core = lax.rem(c, 2)
    x = lax.rem(r, n_x)
    by_factors = p <= FACTOR_SECTIONS - 1
    partner = lax.rem(r + n_x, n_row)

    def place(row):
        return lax.rem(row, n_x) * 2 + lax.div(row, n_x)

    def column(dy, dcore):
        return lax.rem(y + dy, n_y) * 2 + lax.rem(core + dcore, 2)

    up_y, down_y, sibling = column(1, 0), column(n_y - 1, 0), column(0, 1)

    barrier = pltpu.get_barrier_semaphore()

    def greet(d, _):
        pl.semaphore_signal(barrier, inc=1, device_id={"row": lax.rem(r + d, n_row)}, device_id_type=MESH)
        pl.semaphore_signal(barrier, inc=1, device_id={"col": lax.rem(c + d, n_col)}, device_id_type=MESH)
        return 0

    lax.fori_loop(1, n_row, greet, 0)

    @pl.when(p > 0)
    def _():
        for row in (r, partner):
            pl.semaphore_signal(barrier, inc=1, device_id={"pipe": p - 1, "row": row}, device_id_type=MESH)

    @pl.when(p < n_pipe - 1)
    def _():
        for row in (r, partner):
            pl.semaphore_signal(barrier, inc=1, device_id={"pipe": p + 1, "row": row}, device_id_type=MESH)

    xg[r, 0:both, :] = x_ref[...]
    xg[r, both : both + 16, :] = jnp.broadcast_to(gain_ref[...].astype(F32), (16, width)).astype(BF16)
    for i in range(per):
        for which, (ref, cnt) in enumerate(((gate_ref, icnt), (up_ref, icnt), (down_ref, ocnt))):
            live = cnt[c * per + i]
            slot = lax.broadcasted_iota(jnp.int32, (BLK, 2 * BLK), 1) // BLK
            value = ref[i * BLK : (i + 1) * BLK, :].astype(F32)
            wall[c, (i * 3 + which) * BLK : (i * 3 + which + 1) * BLK, :] = jnp.where(slot < live, value, 0.0).astype(BF16)

    @pl.when(p == n_pipe - 1)
    def _():
        for k in range(CHUNKS):
            dyg[k, place(r)] = go_ref[k * tokens : (k + 1) * tokens, :]

    pl.semaphore_wait(barrier, n_row - 1 + n_col - 1 + jnp.where(p > 0, 2, 0) + jnp.where(p < n_pipe - 1, 2, 0))

    def remote(src, dst, send, recv, target):
        return pltpu.make_async_remote_copy(src_ref=src, dst_ref=dst, send_sem=send, recv_sem=recv, device_id=target, device_id_type=MESH)

    def weights(owner, q, target, number):
        share = wall.at[owner, pl.ds(pl.multiple_of(q * piece, piece), piece), :]
        return remote(share, share, wsend.at[number], wrecv.at[owner, q], {"col": target})

    def x_copy(owner, target, number):
        return remote(xg.at[owner], xg.at[owner], xsend.at[number], xrecv.at[owner], {"row": target})

    def dy_copy(k, source, target, number):
        pair = dyg.at[k, pl.ds(source * 2, 2)]
        row = lax.div(r, n_x) * n_x + target
        return remote(pair, pair, gsend.at[k, number], grecv.at[k, source], {"row": row})

    def hop_copy(k, pipe, row, number):
        rows = pl.ds(pl.multiple_of(k * tokens, tokens), tokens)
        return remote(gin_ref.at[rows, :], dyg.at[k, place(r)], hsend.at[k, number], hrecv.at[k, number], {"pipe": pipe, "row": row})

    def swap_copy(k):
        share = dyg.at[k, place(r)]
        return remote(share, share, hsend.at[k, 1], hrecv.at[k, 1], {"row": partner})

    def sum_copy(k, target, source, number):
        return remote(rss.at[k, target], rsr.at[k, source], rsend.at[k, number], rrecv.at[k, source], {"row": target})

    def factor_copy(owner, target, number):
        share = pool.at[pl.ds(pl.multiple_of(owner * span, span), span), :]
        return remote(share, share, asend.at[number], arecv.at[owner], {"col": target})

    def share_start(part, which, k):
        if part < 2:
            return ((part * 3 + which) * n_y + k) * block
        return (6 * n_y + ((part - 2) * 3 + which) * (n_y - 1) + k - 1) * block

    def shares(part, which, k):
        return pl.ds(pl.multiple_of(share_start(part, which, k), block), block)

    def pair_copy(which, k):
        return remote(pool.at[shares(0, which, k), :], pool.at[shares(1, which, k), :], psend.at[which, k], precv.at[which, k], {"col": sibling})

    def ring_copy(which, k, target):
        return remote(pool.at[shares(2, which, k), :], pool.at[shares(3, which, k), :], ysend.at[which, k], yrecv.at[which, k], {"col": target})

    def dh_copy(k, owner, target, number):
        return remote(dhall.at[k, owner], dhall.at[k, owner], dsend.at[k, number], drecv.at[k, owner], {"col": target})

    def xn_copy(target, source, number):
        return remote(xn.at[pl.ds(target * per, per)], xnr.at[source], nsend.at[number], nrecv.at[source], {"col": target})

    def dyc_copy(k, target, source, number):
        return remote(dyg.at[k, place(target)], dyr.at[k, source], csend.at[k, number], crecv.at[k, source], {"col": target})

    def send_dy(k):
        def body(d, _):
            dy_copy(k, x, lax.rem(x + d, n_x), d).start()
            return 0

        lax.fori_loop(1, n_x, body, 0)

    def send_x(d, _):
        x_copy(r, lax.rem(r + d, n_row), d).start()
        return 0

    for q in range(per):
        weights(c, q, up_y, q).start()
        weights(c, (q + 2) % per, down_y, per + q).start()
    lax.fori_loop(1, n_row, send_x, 0)
    for q in range(per):
        weights(c, q, sibling, 8 + q).start()

    @pl.when(p == n_pipe - 1)
    def _():
        def body(k, _):
            swap_copy(k).start()
            return 0

        lax.fori_loop(0, CHUNKS, body, 0)

    for at, ref in ((0, icol_rows), (4, ocol_rows)):
        for row, value in enumerate(slot_table(ref[...])):
            tabv[at + row : at + row + 1, :] = value
    table = pltpu.make_async_copy(tabv, tab, tabsem)
    table.start()
    acc[...] = jnp.zeros_like(acc)
    table.wait()

    rinv[...] = jnp.zeros_like(rinv)

    def squares(d, _):
        owner = lax.rem(r + d, n_row)

        @pl.when(d > 0)
        def _():
            x_copy(owner, owner, 0).wait_recv()

        total = rinv[...]
        for i in range(per):
            value = xg[owner, 0:both, i * BLK : (i + 1) * BLK].astype(F32)
            total = total + value * value
        rinv[...] = total
        return 0

    lax.fori_loop(0, n_row, squares, 0)
    mean = jnp.sum(rinv[...], axis=1, keepdims=True) / features
    rinv[...] = jnp.broadcast_to(lax.rsqrt(mean + EPSILON), (both, BLK))

    def norm(owner, _):
        scale = rinv[...]
        for i in range(per):
            lanes = slice(i * BLK, (i + 1) * BLK)
            gain = xg[owner, both : both + 16, lanes].astype(F32)[0:1, :]
            value = xg[owner, 0:both, lanes].astype(F32)
            xn[owner * per + i] = (value * scale * gain).astype(BF16)
        return 0

    lax.fori_loop(0, n_row, norm, 0)

    def first_dy(k, _):
        swap_copy(k).wait_recv()
        send_dy(k)
        return 0

    @pl.when(p == n_pipe - 1)
    def _():
        lax.fori_loop(0, CHUNKS, first_dy, 0)

    def use(owner, q):
        block_row = owner * per + q
        value = xn[block_row]
        for which, out in ((0, pg), (1, pu)):
            rows = pl.ds(pl.multiple_of(q * piece + which * BLK, BLK), BLK)
            weight = wall[owner, rows, :]
            product = dot(value, weight)
            out[block_row] = product[:, :BLK]
            out[block_rows + block_row] = product[:, BLK:]
            wt[block_row, which * 2 * BLK : (which + 1) * 2 * BLK, :] = weight.T

    turns = (0, 0, 0, 0, n_y - 1, 1, n_y - 1, 1, n_y - 1, 1, n_y - 1, 1, 2, 2, 2, 2)
    quarters = (0, 1, 2, 3, 0, 2, 1, 3, 2, 0, 3, 1, 0, 2, 1, 3)
    steps = len(turns)

    def arrive(s, _):
        @pl.when(s < steps)
        def _():
            q = pick(s, quarters)
            owner = column(pick(s, turns), 0)

            @pl.when(s >= 4)
            def _():
                weights(owner, q, sibling, 0).wait_recv()

                @pl.when(s < 8)
                def _():
                    target = jnp.where(lax.rem(s, 2) == 0, up_y, down_y)
                    weights(owner, q, target, 8 + s).start()

                weights(owner, q, sibling, 12 + s).start()

            use(owner, q)

        @pl.when(s >= 2)
        def _():
            q = pick(s - 2, quarters)
            owner = column(pick(s - 2, turns), 1)
            weights(owner, q, sibling, 0).wait_recv()
            use(owner, q)

        return 0

    lax.fori_loop(0, steps + 2, arrive, 0)

    def add_slots(at, source, rows):
        def body(i, total):
            total = total * tab[at + 1, i].astype(F32) + source[tab[at, i], 0:rows, :]
            sg[i, 0:rows, :] = total
            return total

        lax.fori_loop(0, slots, body, jnp.zeros((rows, BLK), F32), unroll=4 if rows > 64 else 16)

    add_slots(0, pg, both)

    def gates(j, _):
        ab[j] = sg[tab[2, j]] * tab[3, j].astype(F32)
        return 0

    lax.fori_loop(0, blocks, gates, 0)
    add_slots(0, pu, both)

    def hidden(j, _):
        g = ab[j]
        u = sg[tab[2, j]] * tab[3, j].astype(F32)
        s = jax.nn.sigmoid(g)
        a = u * s * (1.0 + g * (1.0 - s))
        b = g * s
        ab[j] = a
        bb[j] = b
        cb[j] = a * g + b * u
        h = (b * u).astype(BF16)
        hb[j] = h

        @pl.when(by_factors)
        def _():
            for which, value in enumerate((g.astype(BF16), u.astype(BF16))):
                pool[pl.ds(pl.multiple_of(c * span + (which * blocks + j) * both, both), both), :] = value

        return 0

    lax.fori_loop(0, blocks, hidden, 0)

    def send_xn(d, _):
        xn_copy(lax.rem(c + d, n_col), c, d).start()
        return 0

    def send_factors():
        for d in range(1, n_y):
            factor_copy(c, column(d, 0), d - 1).start()
        factor_copy(c, sibling, n_y - 1).start()

    def products(k):
        def body(d, _):
            from_x = lax.rem(x + d, n_x)

            @pl.when(d > 0)
            def _():
                dy_copy(k, from_x, from_x, 0).wait_recv()

            for z in range(2):
                owner = z * n_x + from_x
                for i in range(per):
                    block_row = owner * per + i
                    product = dot(dyg[k, from_x * 2 + z, :, i * BLK : (i + 1) * BLK], wall[owner, (i * 3 + 2) * BLK : (i * 3 + 3) * BLK, :])
                    pg[block_row, 0:tokens, :] = product[:, :BLK]
                    pg[block_rows + block_row, 0:tokens, :] = product[:, BLK:]
            return 0

        lax.fori_loop(0, n_x, body, 0)

    def back(k):
        mine = pl.ds(pl.multiple_of(k * tokens, tokens), tokens)
        add_slots(4, pg, tokens)

        def gated(j, total):
            dh = sg[tab[6, j], 0:tokens, :] * tab[7, j].astype(F32)
            dgb[j, mine, :] = (dh * ab[j, mine, :]).astype(BF16)
            dub[j, mine, :] = (dh * bb[j, mine, :]).astype(BF16)
            dhall[k, c, j] = dh.astype(BF16)
            return total + dh * cb[j, mine, :]

        total = lax.fori_loop(0, blocks, gated, jnp.zeros((tokens, BLK), F32), unroll=2)

        @pl.when(by_factors)
        def _():
            for d in range(1, n_y):
                dh_copy(k, c, column(d, 0), d - 1).start()
            dh_copy(k, c, sibling, n_y - 1).start()

        stat = jnp.sum(total, axis=1, keepdims=True)
        high = stat.astype(BF16).astype(F32)
        lane = lax.broadcasted_iota(jnp.int32, (tokens, BLK), 1)
        stat = jnp.where(lane < BLK // 2, high, stat - high).astype(BF16)

        turns = [(1, 2), (1, 1), (1, 3), (0, 2), (1, 0), (0, 1), (0, 3), (0, 0)]
        for group in (turns[:4], turns[4:]):
            owners = [lax.rem(lax.div(r, n_x) + dz, 2) * n_x + lax.rem(x + dx, n_x) for dz, dx in group]
            for owner in owners:
                for i in range(per):
                    block_row = owner * per + i
                    j0, j1 = icol[0, block_row], icol[1, block_row]
                    left = jnp.concatenate([dgb[j0, mine, :], dgb[j1, mine, :], dub[j0, mine, :], dub[j1, mine, :]], axis=1)
                    rss[k, owner, :, i * BLK : (i + 1) * BLK] = dot(left, wt[block_row]).astype(BF16)
                rss[k, owner, :, width : width + BLK] = stat
            for (dz, dx), owner in zip(group, owners):
                if dz or dx:
                    sum_copy(k, owner, r, dz * n_x + dx).start()

        @pl.when(by_factors)
        def _():
            dyr[k, c] = dyg[k, place(c)]

            def send(d, _):
                dyc_copy(k, lax.rem(c + d, n_col), c, d).start()
                return 0

            lax.fori_loop(1, n_col, send, 0)

    def finish(k):
        mine = pl.ds(pl.multiple_of(k * tokens, tokens), tokens)

        total = rss[k, r].astype(F32)
        for d in range(1, n_row):
            owner = lax.rem(r + d, n_row)
            sum_copy(k, owner, owner, 0).wait_recv()
            total = total + rsr[k, owner].astype(F32)
        stat = jnp.sum(total[:, width:], axis=1, keepdims=True) / (BLK // 2)
        scale = rinv[mine, :][:, 0:1]
        gain = xg[r, both : both + 16, :].astype(F32)[0:1, :]
        value = xg[r, mine, :].astype(F32)
        result = dyg[k, place(r)].astype(F32) + gain * scale * total[:, :width]
        result = result - value * (scale * scale * stat / features)
        gin_ref[mine, :] = result.astype(BF16)

        @pl.when(p > 0)
        def _():
            hop_copy(k, p - 1, r, 0).start()
            hop_copy(k, p - 1, partner, 1).start()

    def take_dy(k):
        @pl.when(p < n_pipe - 1)
        def _():
            hop_copy(k, p + 1, r, 0).wait_recv()
            hop_copy(k, p + 1, partner, 1).wait_recv()
            send_dy(k)

    def spread_factors():
        for d in range(1, n_y):
            owner = column(d, 0)
            factor_copy(owner, owner, 0).wait_recv()
            factor_copy(owner, sibling, n_y - 1 + d).start()

    def pass_on(k):
        for d in range(1, n_y):
            owner = column(d, 0)
            dh_copy(k, owner, owner, 0).wait_recv()
            dh_copy(k, owner, sibling, n_y - 1 + d).start()

    def prepare(k):
        mine = pl.ds(pl.multiple_of(k * tokens, tokens), tokens)

        @pl.when(k == 0)
        def _():
            def body(d, _):
                other = lax.rem(c + d, n_col)
                xn_copy(other, other, 0).wait_recv()
                return 0

            lax.fori_loop(1, n_col, body, 0)
            for d in range(n_y):
                factor_copy(column(d, 1), sibling, 0).wait_recv()

        def arrive(d, _):
            other = lax.rem(c + d, n_col)
            dyc_copy(k, other, other, 0).wait_recv()
            return 0

        lax.fori_loop(1, n_col, arrive, 0)

        def body(j, _):
            for o in range(n_col):
                rows = slice(o * tokens, (o + 1) * tokens)
                g, u = (
                    pool[pl.ds(pl.multiple_of(o * span + (which * blocks + j) * both + k * tokens, tokens), tokens), :].astype(F32)
                    for which in range(2)
                )
                s = jax.nn.sigmoid(g)
                b = g * s
                al[j, rows, :] = (u * s * (1.0 + g * (1.0 - s))).astype(BF16)
                bl[j, rows, :] = b.astype(BF16)
                hl[j, rows, :] = (b * u).astype(BF16)
            return 0

        lax.fori_loop(0, blocks, body, 0)
        for i in range(per):
            q0, q1 = ocol[0, c * per + i], ocol[1, c * per + i]
            left = jnp.concatenate([dyr[k, o, :, i * BLK : (i + 1) * BLK] for o in range(n_col)], axis=0).T
            acc[2, i] = acc[2, i] + dot(left, jnp.concatenate([hl[q0], hl[q1]], axis=1))
            xnt[i] = jnp.concatenate([xnr[o, i, mine, :] for o in range(n_col)], axis=0).T

    def grads(k):
        for d in range(n_y):
            dh_copy(k, column(d, 1), sibling, 0).wait_recv()

        def body(j, _):
            dh = jnp.concatenate([dhall[k, o, j] for o in range(n_col)], axis=0).astype(F32)
            dgl[j] = (dh * al[j].astype(F32)).astype(BF16)
            dul[j] = (dh * bl[j].astype(F32)).astype(BF16)
            return 0

        lax.fori_loop(0, blocks, body, 0, unroll=2)
        for i in range(per):
            j0, j1 = icol[0, c * per + i], icol[1, c * per + i]
            acc[0, i] = acc[0, i] + dot(xnt[i], jnp.concatenate([dgl[j0], dgl[j1]], axis=1))
            acc[1, i] = acc[1, i] + dot(xnt[i], jnp.concatenate([dul[j0], dul[j1]], axis=1))

    def own_grads(owner, emit):
        for i in range(per):
            block_row = owner * per + i
            j0, j1 = icol[0, block_row], icol[1, block_row]
            q0, q1 = ocol[0, block_row], ocol[1, block_row]
            left = xn[block_row].T
            emit(0, i, dot(left, jnp.concatenate([dgb[j0], dgb[j1]], axis=1)))
            emit(1, i, dot(left, jnp.concatenate([dub[j0], dub[j1]], axis=1)))
            dy = jnp.concatenate([dyg[k, place(owner), :, i * BLK : (i + 1) * BLK] for k in range(CHUNKS)], axis=0)
            emit(2, i, dot(dy.T, jnp.concatenate([hb[q0], hb[q1]], axis=1)))

    def part_rows(part, which, k, i, s):
        start = share_start(part, which, k) + (i * 2 + s) * BLK
        return pl.ds(pl.multiple_of(start, BLK), BLK)

    def put(part, which, k, i, value):
        for s in range(2):
            pool[part_rows(part, which, k, i, s), :] = value[:, s * BLK : (s + 1) * BLK].astype(BF16)

    def get(part, which, k, i):
        return jnp.concatenate([pool[part_rows(part, which, k, i, s), :] for s in range(2)], axis=1).astype(F32)

    def to_sibling(k, _):
        own_grads(lax.rem(y + k, n_y) * 2 + (1 - core), lambda which, i, value: put(0, which, k, i, value))
        for which in range(3):
            pair_copy(which, k).start()
        return 0

    def to_ring(step, _):
        k = pick(step, (2, 1, 3, 0))
        target = lax.rem(y + k, n_y) * 2 + core
        for which in range(3):
            pair_copy(which, k).wait_recv()

        def emit(which, i, value):
            value = value + get(1, which, k, i)
            acc[which, i] = value

            @pl.when(k > 0)
            def _():
                put(2, which, k, i, value)

        own_grads(target, emit)

        @pl.when(k > 0)
        def _():
            for which in range(3):
                ring_copy(which, k, target).start()

        return 0

    def collect(k, _):
        for which in range(3):
            ring_copy(which, k, sibling).wait_recv()
            for i in range(per):
                acc[which, i] = acc[which, i] + get(3, which, k, i)
        return 0

    @pl.when(by_factors)
    def _():
        xnr[c] = xn[pl.ds(c * per, per)]
        send_factors()
        lax.fori_loop(1, n_col, send_xn, 0)

    @pl.when(p == 0)
    def _():
        spread_factors()

    for k in range(AHEAD):
        take_dy(k)

    def step(s, _):
        @pl.when(s < CHUNKS)
        def _():
            @pl.when(s < CHUNKS - AHEAD)
            def _():
                take_dy(s + AHEAD)

            products(s)
            back(s)

        @pl.when(jnp.logical_and(s == lead, p > 0))
        def _():
            spread_factors()

        @pl.when(jnp.logical_and(s >= lead + 1, s < lead + 1 + CHUNKS))
        def _():
            grads(s - lead - 1)

        @pl.when(jnp.logical_and(s >= lead, s < lead + CHUNKS))
        def _():
            prepare(s - lead)
            pass_on(s - lead)

        @pl.when(jnp.logical_and(s >= LATE, s < CHUNKS + LATE))
        def _():
            finish(s - LATE)

        return 0

    lead = jnp.where(p == 0, FACTORS_LATE, jnp.where(by_factors, CHUNKS + LATE, 3 * CHUNKS))
    lax.fori_loop(0, 2 * CHUNKS + LATE + 1, step, 0)

    @pl.when(jnp.logical_not(by_factors))
    def _():
        lax.fori_loop(0, n_y, to_sibling, 0)
        lax.fori_loop(0, n_y, to_ring, 0)
        lax.fori_loop(1, n_y, collect, 0)

    for i in range(per):
        for which, (ref, cnt) in enumerate(((ggate_ref, icnt), (gup_ref, icnt), (gdown_ref, ocnt))):
            live = cnt[c * per + i]
            slot = lax.broadcasted_iota(jnp.int32, (BLK, 2 * BLK), 1) // BLK
            ref[i * BLK : (i + 1) * BLK, :] = jnp.where(slot < live, acc[which, i], 0.0).astype(BF16)

    def sent_weights(number, _):
        weights(c, 0, sibling, number).wait_send()
        return 0

    lax.fori_loop(0, 28, sent_weights, 0)

    def sent(d, _):
        other = lax.rem(r + d, n_row)
        x_copy(r, other, d).wait_send()
        for k in range(CHUNKS):
            sum_copy(k, other, r, d).wait_send()
        return 0

    lax.fori_loop(1, n_row, sent, 0)

    def sent_dy(d, _):
        for k in range(CHUNKS):
            dy_copy(k, x, lax.rem(x + d, n_x), d).wait_send()
        return 0

    lax.fori_loop(1, n_x, sent_dy, 0)

    @pl.when(p == n_pipe - 1)
    def _():
        for k in range(CHUNKS):
            swap_copy(k).wait_send()

    @pl.when(p > 0)
    def _():
        for k in range(CHUNKS):
            hop_copy(k, p - 1, r, 0).wait_send()
            hop_copy(k, p - 1, partner, 1).wait_send()

    @pl.when(jnp.logical_not(by_factors))
    def _():
        for which in range(3):
            for k in range(n_y):
                pair_copy(which, k).wait_send()
                if k > 0:
                    ring_copy(which, k, sibling).wait_send()

    @pl.when(by_factors)
    def _():
        def sent_beside(d, _):
            beside = lax.rem(c + d, n_col)
            xn_copy(beside, c, d).wait_send()
            for k in range(CHUNKS):
                dyc_copy(k, beside, c, d).wait_send()
            return 0

        lax.fori_loop(1, n_col, sent_beside, 0)

        def sent_factors(number, _):
            factor_copy(c, sibling, number).wait_send()
            for k in range(CHUNKS):
                dh_copy(k, c, sibling, number).wait_send()
            return 0

        lax.fori_loop(0, 2 * n_y - 1, sent_factors, 0)


def hand_over(a, b, c, d, out_a, out_b, out_c, out_d):
    for src, dst in ((a, out_a), (b, out_b), (c, out_c), (d, out_d)):
        dst[...] = src[...]


def local(sizes, inputs, grad_out, norm_gain, gate_weight, up_weight, down_weight, inner_cols, inner_counts, outer_cols, outer_counts):
    n_pipe, n_row, n_y, blocks = sizes
    n_col, n_x = 2 * n_y, n_row // 2
    _, micro, tokens, width = inputs.shape
    both = micro * tokens
    small = both // CHUNKS
    block_rows = width * n_row // BLK
    per = block_rows // n_row
    slots = 2 * block_rows
    rows = gate_weight.shape[1]
    icol, ocol = inner_cols[0].T, outer_cols[0].T
    icnt, ocnt = inner_counts.reshape(block_rows), outer_counts.reshape(block_rows)
    smem = pl.BlockSpec(memory_space=pltpu.SMEM)
    vmem = pl.BlockSpec(memory_space=pltpu.VMEM)
    dma = pltpu.SemaphoreType.DMA
    weight_out = jax.ShapeDtypeStruct((rows, 2 * BLK), BF16)
    outs = (jax.ShapeDtypeStruct((both, width), BF16), weight_out, weight_out, weight_out)
    results = pl.pallas_call(
        functools.partial(main_kernel, sizes),
        out_shape=outs,
        in_specs=[vmem] * 8 + [smem] * 4,
        out_specs=[vmem] * 4,
        scratch_shapes=[
            pltpu.VMEM((n_col, 3 * rows, 2 * BLK), BF16),
            pltpu.VMEM((block_rows, 4 * BLK, BLK), BF16),
            pltpu.VMEM((n_row, both + 16, width), BF16),
            pltpu.VMEM((block_rows, both, BLK), BF16),
            pltpu.VMEM((both, BLK), F32),
            pltpu.VMEM((slots, both, BLK), F32),
            pltpu.VMEM((slots, both, BLK), F32),
            pltpu.VMEM((slots, both, BLK), F32),
            pltpu.VMEM((blocks, both, BLK), F32),
            pltpu.VMEM((blocks, both, BLK), F32),
            pltpu.VMEM((blocks, both, BLK), F32),
            pltpu.VMEM((blocks, both, BLK), BF16),
            pltpu.VMEM((max(n_col * 2 * blocks * both, (12 * n_y - 6) * 2 * rows), BLK), BF16),
            pltpu.VMEM((CHUNKS, n_col, blocks, small, BLK), BF16),
            pltpu.VMEM((blocks, both, BLK), BF16),
            pltpu.VMEM((blocks, both, BLK), BF16),
            pltpu.VMEM((CHUNKS, n_row, small, width), BF16),
            pltpu.VMEM((CHUNKS, n_col, small, width), BF16),
            pltpu.VMEM((n_col, per, both, BLK), BF16),
            pltpu.VMEM((CHUNKS, n_row, small, width + BLK), BF16),
            pltpu.VMEM((CHUNKS, n_row, small, width + BLK), BF16),
            pltpu.VMEM((blocks, n_col * small, BLK), BF16),
            pltpu.VMEM((blocks, n_col * small, BLK), BF16),
            pltpu.VMEM((blocks, n_col * small, BLK), BF16),
            pltpu.VMEM((blocks, n_col * small, BLK), BF16),
            pltpu.VMEM((blocks, n_col * small, BLK), BF16),
            pltpu.VMEM((per, BLK, n_col * small), BF16),
            pltpu.VMEM((3, per, BLK, 2 * BLK), F32),
            pltpu.VMEM((8, BLK), jnp.int32),
            pltpu.SMEM((8, BLK), jnp.int32),
            dma,
            dma((28,)), dma((n_col, per)),
            dma((n_row,)), dma((n_row,)),
            dma((CHUNKS, n_x)), dma((CHUNKS, n_x)),
            dma((CHUNKS, 2)), dma((CHUNKS, 2)),
            dma((CHUNKS, n_row)), dma((CHUNKS, n_row)),
            dma((2 * n_y - 1,)), dma((n_col,)),
            dma((n_col,)), dma((n_col,)),
            dma((CHUNKS, 2 * n_y - 1)), dma((CHUNKS, n_col)),
            dma((CHUNKS, n_col)), dma((CHUNKS, n_col)),
            dma((3, n_y)), dma((3, n_y)),
            dma((3, n_y)), dma((3, n_y)),
        ],
        compiler_params=pltpu.CompilerParams(collective_id=0, has_side_effects=True, vmem_limit_bytes=60 * 1024 * 1024),
        name="backward",
    )(
        inputs.reshape(both, width), grad_out.reshape(both, width), norm_gain,
        gate_weight.reshape(rows, 2 * BLK), up_weight.reshape(rows, 2 * BLK), down_weight.reshape(rows, 2 * BLK),
        icol, ocol, icol, icnt, ocol, ocnt,
    )
    grad_in, gate, up, down = pl.pallas_call(
        hand_over,
        out_shape=outs,
        in_specs=[vmem] * 4,
        out_specs=[vmem] * 4,
        name="hand_over",
    )(*results)
    return grad_in.reshape(inputs.shape), gate[None], up[None], down[None]


def solution(mesh):
    in_specs = (
        P("pipe", None, "col", "row"),
        P(None, "col", "row"),
        P("pipe", "row"),
        P("pipe", "col", "row"),
        P("pipe", "col", "row"),
        P("pipe", "col", "row"),
        P("pipe", None, "row"),
        P("pipe", None, "row"),
        P("pipe", None, "row"),
        P("pipe", None, "row"),
    )
    out_specs = (
        P("pipe", None, "col", "row"),
        P("pipe", "col", "row"),
        P("pipe", "col", "row"),
        P("pipe", "col", "row"),
    )
    sizes = (mesh.shape["pipe"], mesh.shape["row"], mesh.shape["col"] // 2, FF // (mesh.shape["row"] * BLK))
    return jax.shard_map(functools.partial(local, sizes), mesh=mesh, in_specs=in_specs, out_specs=out_specs, check_vma=False)
```

```python
import functools

import jax
import jax.numpy as jnp
from jax import lax
from jax.experimental import pallas as pl
from jax.experimental.pallas import tpu as pltpu
from jax.sharding import PartitionSpec as P

FF = 14336
BLK = 128
EPSILON = 1e-05
MESH = pl.DeviceIdType.MESH
F32 = jnp.float32
BF16 = jnp.bfloat16


CHUNKS = 8
FACTOR_SECTIONS = 2
AHEAD = 1
LATE = 1
SPREAD = 4
FIRST_LATE = 2
FACTORS_LATE = 2


def dot(a, b):
    return jnp.dot(a, b, preferred_element_type=F32)


def pick(index, values):
    result = values[-1]
    for i in reversed(range(len(values) - 1)):
        result = jnp.where(index == i, values[i], result)
    return result


def slot_table(col):
    block_rows = col.shape[1]
    square = (block_rows, block_rows)
    eye = lax.broadcasted_iota(jnp.int32, square, 0) == lax.broadcasted_iota(jnp.int32, square, 1)
    lane = lax.broadcasted_iota(jnp.int32, (1, block_rows), 1)
    down = lax.broadcasted_iota(jnp.int32, (block_rows, BLK), 0)
    place = lax.broadcasted_iota(jnp.int32, (block_rows, BLK), 1)

    def upright(row):
        return jnp.sum(jnp.where(eye, jnp.broadcast_to(row, square), 0), axis=1, keepdims=True)

    rows = [col[s : s + 1, :] for s in range(2)]
    keys = [rows[s] * (2 * block_rows) + s * block_rows + lane for s in range(2)]
    order, keep, upto, count = 0, 0, 0, 0
    for s in range(2):
        key, block = upright(keys[s]), upright(rows[s])
        rank = sum(jnp.sum(jnp.where(keys[t] < key, 1, 0), axis=1, keepdims=True) for t in range(2))
        first = sum(jnp.sum(jnp.where(rows[t] < block, 1, 0), axis=1, keepdims=True) for t in range(2))
        here = rank == place
        order = order + jnp.sum(jnp.where(here, down + s * block_rows, 0), axis=0, keepdims=True)
        keep = keep + jnp.sum(jnp.where(here, jnp.where(rank != first, 1, 0), 0), axis=0, keepdims=True)
        upto = upto + jnp.sum(jnp.where(block <= place, 1, 0), axis=0, keepdims=True)
        count = count + jnp.sum(jnp.where(block == place, 1, 0), axis=0, keepdims=True)
    return order, keep, jnp.maximum(upto - 1, 0), jnp.minimum(count, 1)


def main_kernel(
    sizes,
    x_ref, go_ref, gain_ref, gate_ref, up_ref, down_ref, icol_rows, ocol_rows,
    icol, icnt, ocol, ocnt,
    gin_ref, ggate_ref, gup_ref, gdown_ref,
    wall, wt, xg, xn, rinv, pg, pu, sg, ab, bb, cb, hb, pool, dhall, dgb, dub, dyg, dyr, xnr, rss, rsr, al, bl, hl, dgl, dul, xnt, acc, tabv, tab,
    tabsem, wsend, wrecv, xsend, xrecv, gsend, grecv, hsend, hrecv, rsend, rrecv,
    asend, arecv, nsend, nrecv, dsend, drecv, csend, crecv, psend, precv, ysend, yrecv,
):
    n_pipe, n_row, n_y, blocks = sizes
    n_col, n_x = 2 * n_y, n_row // 2
    both, width = x_ref.shape
    tokens = both // CHUNKS
    features = width * n_row
    block_rows = features // BLK
    per = block_rows // n_row
    slots = 2 * block_rows
    piece = 3 * BLK
    span = 2 * blocks * both
    block = 2 * per * BLK

    p = lax.axis_index("pipe")
    r = lax.axis_index("row")
    c = lax.axis_index("col")
    y = lax.div(c, 2)
    core = lax.rem(c, 2)
    x = lax.rem(r, n_x)
    by_factors = p <= FACTOR_SECTIONS - 1
    partner = lax.rem(r + n_x, n_row)

    def place(row):
        return lax.rem(row, n_x) * 2 + lax.div(row, n_x)

    def column(dy, dcore):
        return lax.rem(y + dy, n_y) * 2 + lax.rem(core + dcore, 2)

    up_y, down_y, sibling = column(1, 0), column(n_y - 1, 0), column(0, 1)

    barrier = pltpu.get_barrier_semaphore()

    def greet(d, _):
        pl.semaphore_signal(barrier, inc=1, device_id={"row": lax.rem(r + d, n_row)}, device_id_type=MESH)
        pl.semaphore_signal(barrier, inc=1, device_id={"col": lax.rem(c + d, n_col)}, device_id_type=MESH)
        return 0

    lax.fori_loop(1, n_row, greet, 0)

    @pl.when(p > 0)
    def _():
        for row in (r, partner):
            pl.semaphore_signal(barrier, inc=1, device_id={"pipe": p - 1, "row": row}, device_id_type=MESH)

    @pl.when(p < n_pipe - 1)
    def _():
        for row in (r, partner):
            pl.semaphore_signal(barrier, inc=1, device_id={"pipe": p + 1, "row": row}, device_id_type=MESH)

    xg[r, 0:both, :] = x_ref[...]
    xg[r, both : both + 16, :] = jnp.broadcast_to(gain_ref[...].astype(F32), (16, width)).astype(BF16)
    for i in range(per):
        for which, (ref, cnt) in enumerate(((gate_ref, icnt), (up_ref, icnt), (down_ref, ocnt))):
            live = cnt[c * per + i]
            slot = lax.broadcasted_iota(jnp.int32, (BLK, 2 * BLK), 1) // BLK
            value = ref[i * BLK : (i + 1) * BLK, :].astype(F32)
            wall[c, (i * 3 + which) * BLK : (i * 3 + which + 1) * BLK, :] = jnp.where(slot < live, value, 0.0).astype(BF16)

    @pl.when(p == n_pipe - 1)
    def _():
        for k in range(CHUNKS):
            dyg[k, place(r)] = go_ref[k * tokens : (k + 1) * tokens, :]

    pl.semaphore_wait(barrier, n_row - 1 + n_col - 1 + jnp.where(p > 0, 2, 0) + jnp.where(p < n_pipe - 1, 2, 0))

    def remote(src, dst, send, recv, target):
        return pltpu.make_async_remote_copy(src_ref=src, dst_ref=dst, send_sem=send, recv_sem=recv, device_id=target, device_id_type=MESH)

    def weights(owner, q, target, number):
        share = wall.at[owner, pl.ds(pl.multiple_of(q * piece, piece), piece), :]
        return remote(share, share, wsend.at[number], wrecv.at[owner, q], {"col": target})

    def x_copy(owner, target, number):
        return remote(xg.at[owner], xg.at[owner], xsend.at[number], xrecv.at[owner], {"row": target})

    def dy_copy(k, source, target, number):
        pair = dyg.at[k, pl.ds(source * 2, 2)]
        row = lax.div(r, n_x) * n_x + target
        return remote(pair, pair, gsend.at[k, number], grecv.at[k, source], {"row": row})

    def hop_copy(k, pipe, row, number):
        rows = pl.ds(pl.multiple_of(k * tokens, tokens), tokens)
        return remote(gin_ref.at[rows, :], dyg.at[k, place(r)], hsend.at[k, number], hrecv.at[k, number], {"pipe": pipe, "row": row})

    def swap_copy(k):
        share = dyg.at[k, place(r)]
        return remote(share, share, hsend.at[k, 1], hrecv.at[k, 1], {"row": partner})

    def sum_copy(k, target, source, number):
        return remote(rss.at[k, target], rsr.at[k, source], rsend.at[k, number], rrecv.at[k, source], {"row": target})

    def factor_copy(owner, target, number):
        share = pool.at[pl.ds(pl.multiple_of(owner * span, span), span), :]
        return remote(share, share, asend.at[number], arecv.at[owner], {"col": target})

    def share_start(part, which, k):
        if part < 2:
            return ((part * 3 + which) * n_y + k) * block
        return (6 * n_y + ((part - 2) * 3 + which) * (n_y - 1) + k - 1) * block

    def shares(part, which, k):
        return pl.ds(pl.multiple_of(share_start(part, which, k), block), block)

    def pair_copy(which, k):
        return remote(pool.at[shares(0, which, k), :], pool.at[shares(1, which, k), :], psend.at[which, k], precv.at[which, k], {"col": sibling})

    def ring_copy(which, k, target):
        return remote(pool.at[shares(2, which, k), :], pool.at[shares(3, which, k), :], ysend.at[which, k], yrecv.at[which, k], {"col": target})

    def far_copy(which, h):
        rows = [pl.ds(pl.multiple_of(share_start(part, which, 2) + h * block // 2, block // 2), block // 2) for part in (2, 3)]
        return remote(pool.at[rows[0], :], pool.at[rows[1], :], ysend.at[which, 2 * h], yrecv.at[which, 2 * h], {"col": (up_y, down_y)[h]})

    def dh_copy(k, owner, target, number):
        return remote(dhall.at[k, owner], dhall.at[k, owner], dsend.at[k, number], drecv.at[k, owner], {"col": target})

    def xn_copy(target, source, number):
        return remote(xn.at[pl.ds(target * per, per)], xnr.at[source], nsend.at[number], nrecv.at[source], {"col": target})

    def dyc_copy(k, target, source, number):
        return remote(dyg.at[k, place(target)], dyr.at[k, source], csend.at[k, number], crecv.at[k, source], {"col": target})

    def send_dy(k):
        def body(d, _):
            dy_copy(k, x, lax.rem(x + d, n_x), d).start()
            return 0

        lax.fori_loop(1, n_x, body, 0)

    def send_x(d, _):
        x_copy(r, lax.rem(r + d, n_row), d).start()
        return 0

    for q in range(per):
        weights(c, q, up_y, q).start()
        weights(c, (q + 2) % per, down_y, per + q).start()
    lax.fori_loop(1, n_row, send_x, 0)
    for q in range(per):
        weights(c, q, sibling, 8 + q).start()

    @pl.when(p == n_pipe - 1)
    def _():
        def body(k, _):
            swap_copy(k).start()
            return 0

        lax.fori_loop(0, CHUNKS, body, 0)

    for at, ref in ((0, icol_rows), (4, ocol_rows)):
        for row, value in enumerate(slot_table(ref[...])):
            tabv[at + row : at + row + 1, :] = value
    table = pltpu.make_async_copy(tabv, tab, tabsem)
    table.start()
    acc[...] = jnp.zeros_like(acc)
    table.wait()

    rinv[...] = jnp.zeros_like(rinv)

    def squares(d, _):
        owner = lax.rem(r + d, n_row)

        @pl.when(d > 0)
        def _():
            x_copy(owner, owner, 0).wait_recv()

        total = rinv[...]
        for i in range(per):
            value = xg[owner, 0:both, i * BLK : (i + 1) * BLK].astype(F32)
            total = total + value * value
        rinv[...] = total
        return 0

    lax.fori_loop(0, n_row, squares, 0)
    mean = jnp.sum(rinv[...], axis=1, keepdims=True) / features
    rinv[...] = jnp.broadcast_to(lax.rsqrt(mean + EPSILON), (both, BLK))

    def norm(owner, _):
        scale = rinv[...]
        for i in range(per):
            lanes = slice(i * BLK, (i + 1) * BLK)
            gain = xg[owner, both : both + 16, lanes].astype(F32)[0:1, :]
            value = xg[owner, 0:both, lanes].astype(F32)
            xn[owner * per + i] = (value * scale * gain).astype(BF16)
        return 0

    lax.fori_loop(0, n_row, norm, 0)

    def first_dy(k, _):
        swap_copy(k).wait_recv()
        send_dy(k)
        return 0

    @pl.when(p == n_pipe - 1)
    def _():
        lax.fori_loop(0, CHUNKS, first_dy, 0)

    def use(owner, q):
        block_row = owner * per + q
        value = xn[block_row]
        for which, out in ((0, pg), (1, pu)):
            rows = pl.ds(pl.multiple_of(q * piece + which * BLK, BLK), BLK)
            weight = wall[owner, rows, :]
            product = dot(value, weight)
            out[block_row] = product[:, :BLK]
            out[block_rows + block_row] = product[:, BLK:]
            wt[block_row, which * 2 * BLK : (which + 1) * 2 * BLK, :] = weight.T

    turns = (0, 0, 0, 0, n_y - 1, 1, n_y - 1, 1, n_y - 1, 1, n_y - 1, 1, 2, 2, 2, 2)
    quarters = (0, 1, 2, 3, 0, 2, 1, 3, 2, 0, 3, 1, 0, 2, 1, 3)
    steps = len(turns)

    def arrive(s, _):
        @pl.when(s < steps)
        def _():
            q = pick(s, quarters)
            owner = column(pick(s, turns), 0)

            @pl.when(s >= 4)
            def _():
                weights(owner, q, sibling, 0).wait_recv()

                @pl.when(s < 8)
                def _():
                    target = jnp.where(lax.rem(s, 2) == 0, up_y, down_y)
                    weights(owner, q, target, 8 + s).start()

                weights(owner, q, sibling, 12 + s).start()

            use(owner, q)

        @pl.when(s >= 2)
        def _():
            q = pick(s - 2, quarters)
            owner = column(pick(s - 2, turns), 1)
            weights(owner, q, sibling, 0).wait_recv()
            use(owner, q)

        return 0

    lax.fori_loop(0, steps + 2, arrive, 0)

    def add_slots(at, source, rows):
        def body(i, total):
            total = total * tab[at + 1, i].astype(F32) + source[tab[at, i], 0:rows, :]
            sg[i, 0:rows, :] = total
            return total

        lax.fori_loop(0, slots, body, jnp.zeros((rows, BLK), F32), unroll=4 if rows > 64 else 16)

    add_slots(0, pg, both)

    def gates(j, _):
        ab[j] = sg[tab[2, j]] * tab[3, j].astype(F32)
        return 0

    lax.fori_loop(0, blocks, gates, 0)
    add_slots(0, pu, both)

    def hidden(j, _):
        g = ab[j]
        u = sg[tab[2, j]] * tab[3, j].astype(F32)
        s = jax.nn.sigmoid(g)
        a = u * s * (1.0 + g * (1.0 - s))
        b = g * s
        ab[j] = a
        bb[j] = b
        cb[j] = a * g + b * u
        h = (b * u).astype(BF16)
        hb[j] = h

        @pl.when(by_factors)
        def _():
            for which, value in enumerate((g.astype(BF16), u.astype(BF16))):
                pool[pl.ds(pl.multiple_of(c * span + (which * blocks + j) * both, both), both), :] = value

        return 0

    lax.fori_loop(0, blocks, hidden, 0)

    def send_xn(d, _):
        xn_copy(lax.rem(c + d, n_col), c, d).start()
        return 0

    def send_factors():
        for d in range(1, n_y):
            factor_copy(c, column(d, 0), d - 1).start()
        factor_copy(c, sibling, n_y - 1).start()

    def products(k):
        def body(d, _):
            from_x = lax.rem(x + d, n_x)

            @pl.when(d > 0)
            def _():
                dy_copy(k, from_x, from_x, 0).wait_recv()

            for z in range(2):
                owner = z * n_x + from_x
                for i in range(per):
                    block_row = owner * per + i
                    product = dot(dyg[k, from_x * 2 + z, :, i * BLK : (i + 1) * BLK], wall[owner, (i * 3 + 2) * BLK : (i * 3 + 3) * BLK, :])
                    pg[block_row, 0:tokens, :] = product[:, :BLK]
                    pg[block_rows + block_row, 0:tokens, :] = product[:, BLK:]
            return 0

        lax.fori_loop(0, n_x, body, 0)

    def back(k):
        mine = pl.ds(pl.multiple_of(k * tokens, tokens), tokens)
        add_slots(4, pg, tokens)

        def gated(j, total):
            dh = sg[tab[6, j], 0:tokens, :] * tab[7, j].astype(F32)
            dgb[j, mine, :] = (dh * ab[j, mine, :]).astype(BF16)
            dub[j, mine, :] = (dh * bb[j, mine, :]).astype(BF16)
            dhall[k, c, j] = dh.astype(BF16)
            return total + dh * cb[j, mine, :]

        total = lax.fori_loop(0, blocks, gated, jnp.zeros((tokens, BLK), F32), unroll=2)

        @pl.when(by_factors)
        def _():
            for d in range(1, n_y):
                dh_copy(k, c, column(d, 0), d - 1).start()
            dh_copy(k, c, sibling, n_y - 1).start()

        stat = jnp.sum(total, axis=1, keepdims=True)
        high = stat.astype(BF16).astype(F32)
        lane = lax.broadcasted_iota(jnp.int32, (tokens, BLK), 1)
        stat = jnp.where(lane < BLK // 2, high, stat - high).astype(BF16)

        turns = [(1, 2), (1, 1), (1, 3), (0, 2), (1, 0), (0, 1), (0, 3), (0, 0)]
        for group in (turns[:4], turns[4:]):
            owners = [lax.rem(lax.div(r, n_x) + dz, 2) * n_x + lax.rem(x + dx, n_x) for dz, dx in group]
            for owner in owners:
                for i in range(per):
                    block_row = owner * per + i
                    j0, j1 = icol[0, block_row], icol[1, block_row]
                    left = jnp.concatenate([dgb[j0, mine, :], dgb[j1, mine, :], dub[j0, mine, :], dub[j1, mine, :]], axis=1)
                    rss[k, owner, :, i * BLK : (i + 1) * BLK] = dot(left, wt[block_row]).astype(BF16)
                rss[k, owner, :, width : width + BLK] = stat
            for (dz, dx), owner in zip(group, owners):
                if dz or dx:
                    sum_copy(k, owner, r, dz * n_x + dx).start()

        @pl.when(by_factors)
        def _():
            dyr[k, c] = dyg[k, place(c)]

            def send(d, _):
                dyc_copy(k, lax.rem(c + d, n_col), c, d).start()
                return 0

            lax.fori_loop(1, n_col, send, 0)

    def finish(k):
        mine = pl.ds(pl.multiple_of(k * tokens, tokens), tokens)

        total = rss[k, r].astype(F32)
        for d in range(1, n_row):
            owner = lax.rem(r + d, n_row)
            sum_copy(k, owner, owner, 0).wait_recv()
            total = total + rsr[k, owner].astype(F32)
        stat = jnp.sum(total[:, width:], axis=1, keepdims=True) / (BLK // 2)
        scale = rinv[mine, :][:, 0:1]
        gain = xg[r, both : both + 16, :].astype(F32)[0:1, :]
        value = xg[r, mine, :].astype(F32)
        result = dyg[k, place(r)].astype(F32) + gain * scale * total[:, :width]
        result = result - value * (scale * scale * stat / features)
        gin_ref[mine, :] = result.astype(BF16)

        @pl.when(p > 0)
        def _():
            hop_copy(k, p - 1, r, 0).start()
            hop_copy(k, p - 1, partner, 1).start()

    def take_dy(k):
        @pl.when(p < n_pipe - 1)
        def _():
            hop_copy(k, p + 1, r, 0).wait_recv()
            hop_copy(k, p + 1, partner, 1).wait_recv()
            send_dy(k)

    def spread_factors():
        for d in range(1, n_y):
            owner = column(d, 0)
            factor_copy(owner, owner, 0).wait_recv()
            factor_copy(owner, sibling, n_y - 1 + d).start()

    def pass_on(k):
        for d in range(1, n_y):
            owner = column(d, 0)
            dh_copy(k, owner, owner, 0).wait_recv()
            dh_copy(k, owner, sibling, n_y - 1 + d).start()

    def prepare(k):
        mine = pl.ds(pl.multiple_of(k * tokens, tokens), tokens)

        @pl.when(k == 0)
        def _():
            def body(d, _):
                other = lax.rem(c + d, n_col)
                xn_copy(other, other, 0).wait_recv()
                return 0

            lax.fori_loop(1, n_col, body, 0)
            for d in range(n_y):
                factor_copy(column(d, 1), sibling, 0).wait_recv()

        def arrive(d, _):
            other = lax.rem(c + d, n_col)
            dyc_copy(k, other, other, 0).wait_recv()
            return 0

        lax.fori_loop(1, n_col, arrive, 0)

        def body(j, _):
            for o in range(n_col):
                rows = slice(o * tokens, (o + 1) * tokens)
                g, u = (
                    pool[pl.ds(pl.multiple_of(o * span + (which * blocks + j) * both + k * tokens, tokens), tokens), :].astype(F32)
                    for which in range(2)
                )
                s = jax.nn.sigmoid(g)
                b = g * s
                al[j, rows, :] = (u * s * (1.0 + g * (1.0 - s))).astype(BF16)
                bl[j, rows, :] = b.astype(BF16)
                hl[j, rows, :] = (b * u).astype(BF16)
            return 0

        lax.fori_loop(0, blocks, body, 0)
        for i in range(per):
            q0, q1 = ocol[0, c * per + i], ocol[1, c * per + i]
            left = jnp.concatenate([dyr[k, o, :, i * BLK : (i + 1) * BLK] for o in range(n_col)], axis=0).T
            acc[2, i] = acc[2, i] + dot(left, jnp.concatenate([hl[q0], hl[q1]], axis=1))
            xnt[i] = jnp.concatenate([xnr[o, i, mine, :] for o in range(n_col)], axis=0).T

    def grads(k):
        for d in range(n_y):
            dh_copy(k, column(d, 1), sibling, 0).wait_recv()

        def body(j, _):
            dh = jnp.concatenate([dhall[k, o, j] for o in range(n_col)], axis=0).astype(F32)
            dgl[j] = (dh * al[j].astype(F32)).astype(BF16)
            dul[j] = (dh * bl[j].astype(F32)).astype(BF16)
            return 0

        lax.fori_loop(0, blocks, body, 0, unroll=2)
        for i in range(per):
            j0, j1 = icol[0, c * per + i], icol[1, c * per + i]
            acc[0, i] = acc[0, i] + dot(xnt[i], jnp.concatenate([dgl[j0], dgl[j1]], axis=1))
            acc[1, i] = acc[1, i] + dot(xnt[i], jnp.concatenate([dul[j0], dul[j1]], axis=1))

    def own_grads(owner, emit):
        for i in range(per):
            block_row = owner * per + i
            j0, j1 = icol[0, block_row], icol[1, block_row]
            q0, q1 = ocol[0, block_row], ocol[1, block_row]
            left = xn[block_row].T
            emit(0, i, dot(left, jnp.concatenate([dgb[j0], dgb[j1]], axis=1)))
            emit(1, i, dot(left, jnp.concatenate([dub[j0], dub[j1]], axis=1)))
            dy = jnp.concatenate([dyg[k, place(owner), :, i * BLK : (i + 1) * BLK] for k in range(CHUNKS)], axis=0)
            emit(2, i, dot(dy.T, jnp.concatenate([hb[q0], hb[q1]], axis=1)))

    def part_rows(part, which, k, i, s):
        start = share_start(part, which, k) + (i * 2 + s) * BLK
        return pl.ds(pl.multiple_of(start, BLK), BLK)

    def put(part, which, k, i, value):
        for s in range(2):
            pool[part_rows(part, which, k, i, s), :] = value[:, s * BLK : (s + 1) * BLK].astype(BF16)

    def get(part, which, k, i):
        return jnp.concatenate([pool[part_rows(part, which, k, i, s), :] for s in range(2)], axis=1).astype(F32)

    def to_sibling(k):
        own_grads(lax.rem(y + k, n_y) * 2 + (1 - core), lambda which, i, value: put(0, which, k, i, value))
        for which in range(3):
            pair_copy(which, k).start()

    def to_ring(k):
        target = lax.rem(y + k, n_y) * 2 + core
        for which in range(3):
            pair_copy(which, k).wait_recv()

        for h in range(2):

            @pl.when(k == 2 * h + 1)
            def _(h=h):
                for which in range(3):
                    far_copy(which, h).wait_recv()

        def emit(which, i, value):
            acc[which, i] = value + get(1, which, k, i)

            @pl.when(k == (1 if i < per // 2 else 3))
            def _():
                acc[which, i] = acc[which, i] + get(3, which, 2, i)

            @pl.when(k > 0)
            def _():
                put(2, which, k, i, acc[which, i])

        own_grads(target, emit)

        @pl.when(k == 2)
        def _():
            for which in range(3):
                for h in range(2):
                    far_copy(which, h).start()

        @pl.when(lax.rem(k, 2) == 1)
        def _():
            for which in range(3):
                ring_copy(which, k, target).start()

    def to_owners(s, _):
        order = (2, 1, 3, 0)

        @pl.when(s < n_y)
        def _():
            to_sibling(pick(s, order))

        @pl.when(s >= 1)
        def _():
            to_ring(pick(s - 1, order))

        return 0

    def collect(side, _):
        k = 2 * side + 1
        for which in range(3):
            ring_copy(which, k, sibling).wait_recv()
            for i in range(per):
                acc[which, i] = acc[which, i] + get(3, which, k, i)
        return 0

    @pl.when(by_factors)
    def _():
        xnr[c] = xn[pl.ds(c * per, per)]
        send_factors()
        lax.fori_loop(1, n_col, send_xn, 0)

    @pl.when(p == 0)
    def _():
        spread_factors()

    for k in range(AHEAD):
        take_dy(k)

    def step(s, _):
        @pl.when(s < CHUNKS)
        def _():
            @pl.when(s < CHUNKS - AHEAD)
            def _():
                take_dy(s + AHEAD)

            products(s)
            back(s)

        @pl.when(jnp.logical_and(s == spread, jnp.logical_and(by_factors, p > 0)))
        def _():
            spread_factors()

        @pl.when(jnp.logical_and(s >= lead, s < lead + CHUNKS))
        def _():
            pass_on(s - lead)

        @pl.when(jnp.logical_and(s >= lead + 1, s < lead + 1 + CHUNKS))
        def _():
            grads(s - lead - 1)

        @pl.when(jnp.logical_and(s >= lead, s < lead + CHUNKS))
        def _():
            prepare(s - lead)

        @pl.when(jnp.logical_and(s >= late, s < CHUNKS + late))
        def _():
            finish(s - late)

        return 0

    late = jnp.where(p == n_pipe - 1, FIRST_LATE, LATE)
    spread = jnp.where(p == 1, SPREAD, CHUNKS + LATE)
    lead = jnp.where(p == 0, FACTORS_LATE, jnp.where(by_factors, CHUNKS + LATE, 3 * CHUNKS))
    lax.fori_loop(0, 2 * CHUNKS + LATE + 1, step, 0)

    @pl.when(jnp.logical_not(by_factors))
    def _():
        lax.fori_loop(0, n_y + 1, to_owners, 0)
        lax.fori_loop(0, 2, collect, 0)

    for i in range(per):
        for which, (ref, cnt) in enumerate(((ggate_ref, icnt), (gup_ref, icnt), (gdown_ref, ocnt))):
            live = cnt[c * per + i]
            slot = lax.broadcasted_iota(jnp.int32, (BLK, 2 * BLK), 1) // BLK
            ref[i * BLK : (i + 1) * BLK, :] = jnp.where(slot < live, acc[which, i], 0.0).astype(BF16)

    def sent_weights(number, _):
        weights(c, 0, sibling, number).wait_send()
        return 0

    lax.fori_loop(0, 28, sent_weights, 0)

    def sent(d, _):
        other = lax.rem(r + d, n_row)
        x_copy(r, other, d).wait_send()
        for k in range(CHUNKS):
            sum_copy(k, other, r, d).wait_send()
        return 0

    lax.fori_loop(1, n_row, sent, 0)

    def sent_dy(d, _):
        for k in range(CHUNKS):
            dy_copy(k, x, lax.rem(x + d, n_x), d).wait_send()
        return 0

    lax.fori_loop(1, n_x, sent_dy, 0)

    @pl.when(p == n_pipe - 1)
    def _():
        for k in range(CHUNKS):
            swap_copy(k).wait_send()

    @pl.when(p > 0)
    def _():
        for k in range(CHUNKS):
            hop_copy(k, p - 1, r, 0).wait_send()
            hop_copy(k, p - 1, partner, 1).wait_send()

    @pl.when(jnp.logical_not(by_factors))
    def _():
        for which in range(3):
            for k in range(n_y):
                pair_copy(which, k).wait_send()
            for h in range(2):
                far_copy(which, h).wait_send()
                ring_copy(which, 2 * h + 1, sibling).wait_send()

    @pl.when(by_factors)
    def _():
        def sent_beside(d, _):
            beside = lax.rem(c + d, n_col)
            xn_copy(beside, c, d).wait_send()
            for k in range(CHUNKS):
                dyc_copy(k, beside, c, d).wait_send()
            return 0

        lax.fori_loop(1, n_col, sent_beside, 0)

        def sent_factors(number, _):
            factor_copy(c, sibling, number).wait_send()
            for k in range(CHUNKS):
                dh_copy(k, c, sibling, number).wait_send()
            return 0

        lax.fori_loop(0, 2 * n_y - 1, sent_factors, 0)


def hand_over(a, b, c, d, out_a, out_b, out_c, out_d):
    for src, dst in ((a, out_a), (b, out_b), (c, out_c), (d, out_d)):
        dst[...] = src[...]


def local(sizes, inputs, grad_out, norm_gain, gate_weight, up_weight, down_weight, inner_cols, inner_counts, outer_cols, outer_counts):
    n_pipe, n_row, n_y, blocks = sizes
    n_col, n_x = 2 * n_y, n_row // 2
    _, micro, tokens, width = inputs.shape
    both = micro * tokens
    small = both // CHUNKS
    block_rows = width * n_row // BLK
    per = block_rows // n_row
    slots = 2 * block_rows
    rows = gate_weight.shape[1]
    icol, ocol = inner_cols[0].T, outer_cols[0].T
    icnt, ocnt = inner_counts.reshape(block_rows), outer_counts.reshape(block_rows)
    smem = pl.BlockSpec(memory_space=pltpu.SMEM)
    vmem = pl.BlockSpec(memory_space=pltpu.VMEM)
    dma = pltpu.SemaphoreType.DMA
    weight_out = jax.ShapeDtypeStruct((rows, 2 * BLK), BF16)
    outs = (jax.ShapeDtypeStruct((both, width), BF16), weight_out, weight_out, weight_out)
    results = pl.pallas_call(
        functools.partial(main_kernel, sizes),
        out_shape=outs,
        in_specs=[vmem] * 8 + [smem] * 4,
        out_specs=[vmem] * 4,
        scratch_shapes=[
            pltpu.VMEM((n_col, 3 * rows, 2 * BLK), BF16),
            pltpu.VMEM((block_rows, 4 * BLK, BLK), BF16),
            pltpu.VMEM((n_row, both + 16, width), BF16),
            pltpu.VMEM((block_rows, both, BLK), BF16),
            pltpu.VMEM((both, BLK), F32),
            pltpu.VMEM((slots, both, BLK), F32),
            pltpu.VMEM((slots, both, BLK), F32),
            pltpu.VMEM((slots, both, BLK), F32),
            pltpu.VMEM((blocks, both, BLK), F32),
            pltpu.VMEM((blocks, both, BLK), F32),
            pltpu.VMEM((blocks, both, BLK), F32),
            pltpu.VMEM((blocks, both, BLK), BF16),
            pltpu.VMEM((max(n_col * 2 * blocks * both, (12 * n_y - 6) * 2 * rows), BLK), BF16),
            pltpu.VMEM((CHUNKS, n_col, blocks, small, BLK), BF16),
            pltpu.VMEM((blocks, both, BLK), BF16),
            pltpu.VMEM((blocks, both, BLK), BF16),
            pltpu.VMEM((CHUNKS, n_row, small, width), BF16),
            pltpu.VMEM((CHUNKS, n_col, small, width), BF16),
            pltpu.VMEM((n_col, per, both, BLK), BF16),
            pltpu.VMEM((CHUNKS, n_row, small, width + BLK), BF16),
            pltpu.VMEM((CHUNKS, n_row, small, width + BLK), BF16),
            pltpu.VMEM((blocks, n_col * small, BLK), BF16),
            pltpu.VMEM((blocks, n_col * small, BLK), BF16),
            pltpu.VMEM((blocks, n_col * small, BLK), BF16),
            pltpu.VMEM((blocks, n_col * small, BLK), BF16),
            pltpu.VMEM((blocks, n_col * small, BLK), BF16),
            pltpu.VMEM((per, BLK, n_col * small), BF16),
            pltpu.VMEM((3, per, BLK, 2 * BLK), F32),
            pltpu.VMEM((8, BLK), jnp.int32),
            pltpu.SMEM((8, BLK), jnp.int32),
            dma,
            dma((28,)), dma((n_col, per)),
            dma((n_row,)), dma((n_row,)),
            dma((CHUNKS, n_x)), dma((CHUNKS, n_x)),
            dma((CHUNKS, 2)), dma((CHUNKS, 2)),
            dma((CHUNKS, n_row)), dma((CHUNKS, n_row)),
            dma((2 * n_y - 1,)), dma((n_col,)),
            dma((n_col,)), dma((n_col,)),
            dma((CHUNKS, 2 * n_y - 1)), dma((CHUNKS, n_col)),
            dma((CHUNKS, n_col)), dma((CHUNKS, n_col)),
            dma((3, n_y)), dma((3, n_y)),
            dma((3, n_y)), dma((3, n_y)),
        ],
        compiler_params=pltpu.CompilerParams(collective_id=0, has_side_effects=True, vmem_limit_bytes=60 * 1024 * 1024),
        name="backward",
    )(
        inputs.reshape(both, width), grad_out.reshape(both, width), norm_gain,
        gate_weight.reshape(rows, 2 * BLK), up_weight.reshape(rows, 2 * BLK), down_weight.reshape(rows, 2 * BLK),
        icol, ocol, icol, icnt, ocol, ocnt,
    )
    grad_in, gate, up, down = pl.pallas_call(
        hand_over,
        out_shape=outs,
        in_specs=[vmem] * 4,
        out_specs=[vmem] * 4,
        name="hand_over",
    )(*results)
    return grad_in.reshape(inputs.shape), gate[None], up[None], down[None]


def solution(mesh):
    in_specs = (
        P("pipe", None, "col", "row"),
        P(None, "col", "row"),
        P("pipe", "row"),
        P("pipe", "col", "row"),
        P("pipe", "col", "row"),
        P("pipe", "col", "row"),
        P("pipe", None, "row"),
        P("pipe", None, "row"),
        P("pipe", None, "row"),
        P("pipe", None, "row"),
    )
    out_specs = (
        P("pipe", None, "col", "row"),
        P("pipe", "col", "row"),
        P("pipe", "col", "row"),
        P("pipe", "col", "row"),
    )
    sizes = (mesh.shape["pipe"], mesh.shape["row"], mesh.shape["col"] // 2, FF // (mesh.shape["row"] * BLK))
    return jax.shard_map(functools.partial(local, sizes), mesh=mesh, in_specs=in_specs, out_specs=out_specs, check_vma=False)
```

```python
import functools

import jax
import jax.numpy as jnp
from jax import lax
from jax.experimental import pallas as pl
from jax.experimental.pallas import tpu as pltpu
from jax.sharding import PartitionSpec as P

FF = 14336
BLK = 128
EPSILON = 1e-05
MESH = pl.DeviceIdType.MESH
F32 = jnp.float32
BF16 = jnp.bfloat16


CHUNKS = 8
FACTOR_SECTIONS = 2
AHEAD = 1
LATE = 1
SPREAD = 4
FIRST_LATE = 2
FACTORS_LATE = 2


def dot(a, b):
    return jnp.dot(a, b, preferred_element_type=F32)


def pick(index, values):
    result = values[-1]
    for i in reversed(range(len(values) - 1)):
        result = jnp.where(index == i, values[i], result)
    return result


def slot_table(col):
    block_rows = col.shape[1]
    square = (block_rows, block_rows)
    eye = lax.broadcasted_iota(jnp.int32, square, 0) == lax.broadcasted_iota(jnp.int32, square, 1)
    lane = lax.broadcasted_iota(jnp.int32, (1, block_rows), 1)
    down = lax.broadcasted_iota(jnp.int32, (block_rows, BLK), 0)
    place = lax.broadcasted_iota(jnp.int32, (block_rows, BLK), 1)

    def upright(row):
        return jnp.sum(jnp.where(eye, jnp.broadcast_to(row, square), 0), axis=1, keepdims=True)

    rows = [col[s : s + 1, :] for s in range(2)]
    keys = [rows[s] * (2 * block_rows) + s * block_rows + lane for s in range(2)]
    order, keep, upto, count = 0, 0, 0, 0
    for s in range(2):
        key, block = upright(keys[s]), upright(rows[s])
        rank = sum(jnp.sum(jnp.where(keys[t] < key, 1, 0), axis=1, keepdims=True) for t in range(2))
        first = sum(jnp.sum(jnp.where(rows[t] < block, 1, 0), axis=1, keepdims=True) for t in range(2))
        here = rank == place
        order = order + jnp.sum(jnp.where(here, down + s * block_rows, 0), axis=0, keepdims=True)
        keep = keep + jnp.sum(jnp.where(here, jnp.where(rank != first, 1, 0), 0), axis=0, keepdims=True)
        upto = upto + jnp.sum(jnp.where(block <= place, 1, 0), axis=0, keepdims=True)
        count = count + jnp.sum(jnp.where(block == place, 1, 0), axis=0, keepdims=True)
    return order, keep, jnp.maximum(upto - 1, 0), jnp.minimum(count, 1)


def main_kernel(
    sizes,
    x_ref, go_ref, gain_ref, gate_ref, up_ref, down_ref, icol_rows, ocol_rows,
    icol, icnt, ocol, ocnt,
    gin_ref, ggate_ref, gup_ref, gdown_ref,
    wall, wt, xg, xn, rinv, pg, pu, sg, ab, bb, cb, hb, pool, dhall, dgb, dub, dyg, dyr, xnr, rss, rsr, al, bl, hl, dgl, dul, xnt, acc, tabv, tab, held,
    heldsem, tabsem, wsend, wrecv, xsend, xrecv, gsend, grecv, hsend, hrecv, rsend, rrecv,
    asend, arecv, nsend, nrecv, dsend, drecv, csend, crecv, psend, precv, ysend, yrecv,
):
    n_pipe, n_row, n_y, blocks = sizes
    n_col, n_x = 2 * n_y, n_row // 2
    both, width = x_ref.shape
    tokens = both // CHUNKS
    features = width * n_row
    block_rows = features // BLK
    per = block_rows // n_row
    slots = 2 * block_rows
    piece = 3 * BLK
    span = 2 * blocks * both
    block = 2 * per * BLK

    p = lax.axis_index("pipe")
    r = lax.axis_index("row")
    c = lax.axis_index("col")
    y = lax.div(c, 2)
    core = lax.rem(c, 2)
    x = lax.rem(r, n_x)
    by_factors = p <= FACTOR_SECTIONS - 1
    partner = lax.rem(r + n_x, n_row)

    def place(row):
        return lax.rem(row, n_x) * 2 + lax.div(row, n_x)

    def column(dy, dcore):
        return lax.rem(y + dy, n_y) * 2 + lax.rem(core + dcore, 2)

    up_y, down_y, sibling = column(1, 0), column(n_y - 1, 0), column(0, 1)

    barrier = pltpu.get_barrier_semaphore()

    def greet(d, _):
        pl.semaphore_signal(barrier, inc=1, device_id={"row": lax.rem(r + d, n_row)}, device_id_type=MESH)
        pl.semaphore_signal(barrier, inc=1, device_id={"col": lax.rem(c + d, n_col)}, device_id_type=MESH)
        return 0

    lax.fori_loop(1, n_row, greet, 0)

    @pl.when(p > 0)
    def _():
        for row in (r, partner):
            pl.semaphore_signal(barrier, inc=1, device_id={"pipe": p - 1, "row": row}, device_id_type=MESH)

    @pl.when(p < n_pipe - 1)
    def _():
        for row in (r, partner):
            pl.semaphore_signal(barrier, inc=1, device_id={"pipe": p + 1, "row": row}, device_id_type=MESH)

    fetches = [pltpu.make_async_copy(src, held.at[i], heldsem.at[i]) for i, src in enumerate((gate_ref, up_ref, down_ref))]
    for fetch in fetches:
        fetch.start()
    xg[r, 0:both, :] = x_ref[...]
    xg[r, both : both + 16, :] = jnp.broadcast_to(gain_ref[...].astype(F32), (16, width)).astype(BF16)
    for which, cnt in enumerate((icnt, icnt, ocnt)):
        fetches[which].wait()
        for i in range(per):
            live = cnt[c * per + i]
            slot = lax.broadcasted_iota(jnp.int32, (BLK, 2 * BLK), 1) // BLK
            value = held[which, i * BLK : (i + 1) * BLK, :].astype(F32)
            wall[c, (i * 3 + which) * BLK : (i * 3 + which + 1) * BLK, :] = jnp.where(slot < live, value, 0.0).astype(BF16)

    @pl.when(p == n_pipe - 1)
    def _():
        for k in range(CHUNKS):
            dyg[k, place(r)] = go_ref[k * tokens : (k + 1) * tokens, :]

    pl.semaphore_wait(barrier, n_row - 1 + n_col - 1 + jnp.where(p > 0, 2, 0) + jnp.where(p < n_pipe - 1, 2, 0))

    def remote(src, dst, send, recv, target):
        return pltpu.make_async_remote_copy(src_ref=src, dst_ref=dst, send_sem=send, recv_sem=recv, device_id=target, device_id_type=MESH)

    def weights(owner, q, target, number):
        share = wall.at[owner, pl.ds(pl.multiple_of(q * piece, piece), piece), :]
        return remote(share, share, wsend.at[number], wrecv.at[owner, q], {"col": target})

    def x_copy(owner, target, number):
        return remote(xg.at[owner], xg.at[owner], xsend.at[number], xrecv.at[owner], {"row": target})

    def dy_copy(k, source, target, number):
        pair = dyg.at[k, pl.ds(source * 2, 2)]
        row = lax.div(r, n_x) * n_x + target
        return remote(pair, pair, gsend.at[k, number], grecv.at[k, source], {"row": row})

    def hop_copy(k, pipe, row, number):
        rows = pl.ds(pl.multiple_of(k * tokens, tokens), tokens)
        return remote(gin_ref.at[rows, :], dyg.at[k, place(r)], hsend.at[k, number], hrecv.at[k, number], {"pipe": pipe, "row": row})

    def swap_copy(k):
        share = dyg.at[k, place(r)]
        return remote(share, share, hsend.at[k, 1], hrecv.at[k, 1], {"row": partner})

    def sum_copy(k, target, source, number):
        return remote(rss.at[k, target], rsr.at[k, source], rsend.at[k, number], rrecv.at[k, source], {"row": target})

    def factor_copy(owner, target, number):
        share = pool.at[pl.ds(pl.multiple_of(owner * span, span), span), :]
        return remote(share, share, asend.at[number], arecv.at[owner], {"col": target})

    def share_start(part, which, k):
        if part < 2:
            return ((part * 3 + which) * n_y + k) * block
        return (6 * n_y + ((part - 2) * 3 + which) * (n_y - 1) + k - 1) * block

    def shares(part, which, k):
        return pl.ds(pl.multiple_of(share_start(part, which, k), block), block)

    def pair_copy(which, k):
        return remote(pool.at[shares(0, which, k), :], pool.at[shares(1, which, k), :], psend.at[which, k], precv.at[which, k], {"col": sibling})

    def ring_copy(which, k, target):
        return remote(pool.at[shares(2, which, k), :], pool.at[shares(3, which, k), :], ysend.at[which, k], yrecv.at[which, k], {"col": target})

    def far_copy(which, h):
        rows = [pl.ds(pl.multiple_of(share_start(part, which, 2) + h * block // 2, block // 2), block // 2) for part in (2, 3)]
        return remote(pool.at[rows[0], :], pool.at[rows[1], :], ysend.at[which, 2 * h], yrecv.at[which, 2 * h], {"col": (up_y, down_y)[h]})

    def dh_copy(k, owner, target, number):
        return remote(dhall.at[k, owner], dhall.at[k, owner], dsend.at[k, number], drecv.at[k, owner], {"col": target})

    def xn_copy(target, source, number):
        return remote(xn.at[pl.ds(target * per, per)], xnr.at[source], nsend.at[number], nrecv.at[source], {"col": target})

    def dyc_copy(k, target, source, number):
        return remote(dyg.at[k, place(target)], dyr.at[k, source], csend.at[k, number], crecv.at[k, source], {"col": target})

    def send_dy(k):
        for d in (2, 1, 3):
            dy_copy(k, x, lax.rem(x + d, n_x), d).start()

    def send_x(d, _):
        x_copy(r, lax.rem(r + d, n_row), d).start()
        return 0

    for q in range(per):
        weights(c, q, up_y, q).start()
        weights(c, (q + 2) % per, down_y, per + q).start()
    lax.fori_loop(1, n_row, send_x, 0)
    for q in range(per):
        weights(c, q, sibling, 8 + q).start()

    @pl.when(p == n_pipe - 1)
    def _():
        def body(k, _):
            swap_copy(k).start()
            return 0

        lax.fori_loop(0, CHUNKS, body, 0)

    for at, ref in ((0, icol_rows), (4, ocol_rows)):
        for row, value in enumerate(slot_table(ref[...])):
            tabv[at + row : at + row + 1, :] = value
    table = pltpu.make_async_copy(tabv, tab, tabsem)
    table.start()
    acc[...] = jnp.zeros_like(acc)
    table.wait()

    rinv[...] = jnp.zeros_like(rinv)

    def squares(d, _):
        owner = lax.rem(r + d, n_row)

        @pl.when(d > 0)
        def _():
            x_copy(owner, owner, 0).wait_recv()

        total = rinv[...]
        for i in range(per):
            value = xg[owner, 0:both, i * BLK : (i + 1) * BLK].astype(F32)
            total = total + value * value
        rinv[...] = total
        return 0

    lax.fori_loop(0, n_row, squares, 0)
    mean = jnp.sum(rinv[...], axis=1, keepdims=True) / features
    rinv[...] = jnp.broadcast_to(lax.rsqrt(mean + EPSILON), (both, BLK))

    def norm(owner, _):
        scale = rinv[...]
        for i in range(per):
            lanes = slice(i * BLK, (i + 1) * BLK)
            gain = xg[owner, both : both + 16, lanes].astype(F32)[0:1, :]
            value = xg[owner, 0:both, lanes].astype(F32)
            xn[owner * per + i] = (value * scale * gain).astype(BF16)
        return 0

    lax.fori_loop(0, n_row, norm, 0)

    def first_dy(k, _):
        swap_copy(k).wait_recv()
        send_dy(k)
        return 0

    @pl.when(p == n_pipe - 1)
    def _():
        lax.fori_loop(0, CHUNKS, first_dy, 0)

    def use(owner, q):
        block_row = owner * per + q
        value = xn[block_row]
        for which, out in ((0, pg), (1, pu)):
            rows = pl.ds(pl.multiple_of(q * piece + which * BLK, BLK), BLK)
            weight = wall[owner, rows, :]
            product = dot(value, weight)
            out[block_row] = product[:, :BLK]
            out[block_rows + block_row] = product[:, BLK:]
            wt[block_row, which * 2 * BLK : (which + 1) * 2 * BLK, :] = weight.T

    turns = (0, 0, 0, 0, n_y - 1, 1, n_y - 1, 1, n_y - 1, 1, n_y - 1, 1, 2, 2, 2, 2)
    quarters = (0, 1, 2, 3, 0, 2, 1, 3, 2, 0, 3, 1, 0, 2, 1, 3)
    steps = len(turns)

    def arrive(s, _):
        @pl.when(s < steps)
        def _():
            q = pick(s, quarters)
            owner = column(pick(s, turns), 0)

            @pl.when(s >= 4)
            def _():
                weights(owner, q, sibling, 0).wait_recv()

                @pl.when(s < 8)
                def _():
                    target = jnp.where(lax.rem(s, 2) == 0, up_y, down_y)
                    weights(owner, q, target, 8 + s).start()

                weights(owner, q, sibling, 12 + s).start()

            use(owner, q)

        @pl.when(s >= 2)
        def _():
            q = pick(s - 2, quarters)
            owner = column(pick(s - 2, turns), 1)
            weights(owner, q, sibling, 0).wait_recv()
            use(owner, q)

        return 0

    lax.fori_loop(0, steps + 2, arrive, 0)

    def add_slots(at, source, rows):
        def body(i, total):
            total = total * tab[at + 1, i].astype(F32) + source[tab[at, i], 0:rows, :]
            sg[i, 0:rows, :] = total
            return total

        lax.fori_loop(0, slots, body, jnp.zeros((rows, BLK), F32), unroll=4 if rows > 64 else 16)

    add_slots(0, pg, both)

    def gates(j, _):
        ab[j] = sg[tab[2, j]] * tab[3, j].astype(F32)
        return 0

    lax.fori_loop(0, blocks, gates, 0)
    add_slots(0, pu, both)

    def hidden(j, _):
        g = ab[j]
        u = sg[tab[2, j]] * tab[3, j].astype(F32)
        s = jax.nn.sigmoid(g)
        a = u * s * (1.0 + g * (1.0 - s))
        b = g * s
        ab[j] = a
        bb[j] = b
        cb[j] = a * g + b * u
        h = (b * u).astype(BF16)
        hb[j] = h

        @pl.when(by_factors)
        def _():
            for which, value in enumerate((g.astype(BF16), u.astype(BF16))):
                pool[pl.ds(pl.multiple_of(c * span + (which * blocks + j) * both, both), both), :] = value

        return 0

    lax.fori_loop(0, blocks, hidden, 0)

    def send_xn(d, _):
        xn_copy(lax.rem(c + d, n_col), c, d).start()
        return 0

    def send_factors():
        for d in range(1, n_y):
            factor_copy(c, column(d, 0), d - 1).start()
        factor_copy(c, sibling, n_y - 1).start()

    def products(k):
        def body(d, _):
            from_x = lax.rem(x + pick(d, (0, 1, 3, 2)), n_x)

            @pl.when(d > 0)
            def _():
                dy_copy(k, from_x, from_x, 0).wait_recv()

            for z in range(2):
                owner = z * n_x + from_x
                for i in range(per):
                    block_row = owner * per + i
                    product = dot(dyg[k, from_x * 2 + z, :, i * BLK : (i + 1) * BLK], wall[owner, (i * 3 + 2) * BLK : (i * 3 + 3) * BLK, :])
                    pg[block_row, 0:tokens, :] = product[:, :BLK]
                    pg[block_rows + block_row, 0:tokens, :] = product[:, BLK:]
            return 0

        lax.fori_loop(0, n_x, body, 0)

    def back(k):
        mine = pl.ds(pl.multiple_of(k * tokens, tokens), tokens)
        add_slots(4, pg, tokens)

        def gated(j, total):
            dh = sg[tab[6, j], 0:tokens, :] * tab[7, j].astype(F32)
            dgb[j, mine, :] = (dh * ab[j, mine, :]).astype(BF16)
            dub[j, mine, :] = (dh * bb[j, mine, :]).astype(BF16)
            dhall[k, c, j] = dh.astype(BF16)
            return total + dh * cb[j, mine, :]

        total = lax.fori_loop(0, blocks, gated, jnp.zeros((tokens, BLK), F32), unroll=2)

        @pl.when(by_factors)
        def _():
            for d in range(1, n_y):
                dh_copy(k, c, column(d, 0), d - 1).start()
            dh_copy(k, c, sibling, n_y - 1).start()

        stat = jnp.sum(total, axis=1, keepdims=True)
        high = stat.astype(BF16).astype(F32)
        lane = lax.broadcasted_iota(jnp.int32, (tokens, BLK), 1)
        stat = jnp.where(lane < BLK // 2, high, stat - high).astype(BF16)

        turns = [(1, 2), (1, 1), (1, 3), (0, 2), (1, 0), (0, 1), (0, 3), (0, 0)]
        for group in (turns[:4], turns[4:]):
            owners = [lax.rem(lax.div(r, n_x) + dz, 2) * n_x + lax.rem(x + dx, n_x) for dz, dx in group]
            for owner in owners:
                for i in range(per):
                    block_row = owner * per + i
                    j0, j1 = icol[0, block_row], icol[1, block_row]
                    left = jnp.concatenate([dgb[j0, mine, :], dgb[j1, mine, :], dub[j0, mine, :], dub[j1, mine, :]], axis=1)
                    rss[k, owner, :, i * BLK : (i + 1) * BLK] = dot(left, wt[block_row]).astype(BF16)
                rss[k, owner, :, width : width + BLK] = stat
            for (dz, dx), owner in zip(group, owners):
                if dz or dx:
                    sum_copy(k, owner, r, dz * n_x + dx).start()

        @pl.when(by_factors)
        def _():
            dyr[k, c] = dyg[k, place(c)]

            def send(d, _):
                dyc_copy(k, lax.rem(c + d, n_col), c, d).start()
                return 0

            lax.fori_loop(1, n_col, send, 0)

    def finish(k):
        mine = pl.ds(pl.multiple_of(k * tokens, tokens), tokens)

        total = rss[k, r].astype(F32)
        for d in range(1, n_row):
            owner = lax.rem(r + d, n_row)
            sum_copy(k, owner, owner, 0).wait_recv()
            total = total + rsr[k, owner].astype(F32)
        stat = jnp.sum(total[:, width:], axis=1, keepdims=True) / (BLK // 2)
        scale = rinv[mine, :][:, 0:1]
        gain = xg[r, both : both + 16, :].astype(F32)[0:1, :]
        value = xg[r, mine, :].astype(F32)
        result = dyg[k, place(r)].astype(F32) + gain * scale * total[:, :width]
        result = result - value * (scale * scale * stat / features)
        gin_ref[mine, :] = result.astype(BF16)

        @pl.when(p > 0)
        def _():
            hop_copy(k, p - 1, r, 0).start()
            hop_copy(k, p - 1, partner, 1).start()

    def take_dy(k):
        @pl.when(p < n_pipe - 1)
        def _():
            hop_copy(k, p + 1, r, 0).wait_recv()
            hop_copy(k, p + 1, partner, 1).wait_recv()
            send_dy(k)

    def spread_factors():
        for d in range(1, n_y):
            owner = column(d, 0)
            factor_copy(owner, owner, 0).wait_recv()
            factor_copy(owner, sibling, n_y - 1 + d).start()

    def pass_on(k):
        for d in range(1, n_y):
            owner = column(d, 0)
            dh_copy(k, owner, owner, 0).wait_recv()
            dh_copy(k, owner, sibling, n_y - 1 + d).start()

    def prepare(k):
        mine = pl.ds(pl.multiple_of(k * tokens, tokens), tokens)

        @pl.when(k == 0)
        def _():
            def body(d, _):
                other = lax.rem(c + d, n_col)
                xn_copy(other, other, 0).wait_recv()
                return 0

            lax.fori_loop(1, n_col, body, 0)
            for d in range(n_y):
                factor_copy(column(d, 1), sibling, 0).wait_recv()

        def arrive(d, _):
            other = lax.rem(c + d, n_col)
            dyc_copy(k, other, other, 0).wait_recv()
            return 0

        lax.fori_loop(1, n_col, arrive, 0)

        def body(j, _):
            for o in range(n_col):
                rows = slice(o * tokens, (o + 1) * tokens)
                g, u = (
                    pool[pl.ds(pl.multiple_of(o * span + (which * blocks + j) * both + k * tokens, tokens), tokens), :].astype(F32)
                    for which in range(2)
                )
                s = jax.nn.sigmoid(g)
                b = g * s
                al[j, rows, :] = (u * s * (1.0 + g * (1.0 - s))).astype(BF16)
                bl[j, rows, :] = b.astype(BF16)
                hl[j, rows, :] = (b * u).astype(BF16)
            return 0

        lax.fori_loop(0, blocks, body, 0)
        for i in range(per):
            q0, q1 = ocol[0, c * per + i], ocol[1, c * per + i]
            left = jnp.concatenate([dyr[k, o, :, i * BLK : (i + 1) * BLK] for o in range(n_col)], axis=0).T
            acc[2, i] = acc[2, i] + dot(left, jnp.concatenate([hl[q0], hl[q1]], axis=1))
            xnt[i] = jnp.concatenate([xnr[o, i, mine, :] for o in range(n_col)], axis=0).T

    def grads(k):
        for d in range(n_y):
            dh_copy(k, column(d, 1), sibling, 0).wait_recv()

        def body(j, _):
            dh = jnp.concatenate([dhall[k, o, j] for o in range(n_col)], axis=0).astype(F32)
            dgl[j] = (dh * al[j].astype(F32)).astype(BF16)
            dul[j] = (dh * bl[j].astype(F32)).astype(BF16)
            return 0

        lax.fori_loop(0, blocks, body, 0, unroll=2)
        for i in range(per):
            j0, j1 = icol[0, c * per + i], icol[1, c * per + i]
            acc[0, i] = acc[0, i] + dot(xnt[i], jnp.concatenate([dgl[j0], dgl[j1]], axis=1))
            acc[1, i] = acc[1, i] + dot(xnt[i], jnp.concatenate([dul[j0], dul[j1]], axis=1))

    def own_grads(owner, emit):
        for i in range(per):
            block_row = owner * per + i
            j0, j1 = icol[0, block_row], icol[1, block_row]
            q0, q1 = ocol[0, block_row], ocol[1, block_row]
            left = xn[block_row].T
            emit(0, i, dot(left, jnp.concatenate([dgb[j0], dgb[j1]], axis=1)))
            emit(1, i, dot(left, jnp.concatenate([dub[j0], dub[j1]], axis=1)))
            dy = jnp.concatenate([dyg[k, place(owner), :, i * BLK : (i + 1) * BLK] for k in range(CHUNKS)], axis=0)
            emit(2, i, dot(dy.T, jnp.concatenate([hb[q0], hb[q1]], axis=1)))

    def part_rows(part, which, k, i, s):
        start = share_start(part, which, k) + (i * 2 + s) * BLK
        return pl.ds(pl.multiple_of(start, BLK), BLK)

    def put(part, which, k, i, value):
        for s in range(2):
            pool[part_rows(part, which, k, i, s), :] = value[:, s * BLK : (s + 1) * BLK].astype(BF16)

    def get(part, which, k, i):
        return jnp.concatenate([pool[part_rows(part, which, k, i, s), :] for s in range(2)], axis=1).astype(F32)

    def to_sibling(k):
        own_grads(lax.rem(y + k, n_y) * 2 + (1 - core), lambda which, i, value: put(0, which, k, i, value))
        for which in range(3):
            pair_copy(which, k).start()

    def to_ring(k):
        target = lax.rem(y + k, n_y) * 2 + core
        for which in range(3):
            pair_copy(which, k).wait_recv()

        for h in range(2):

            @pl.when(k == 2 * h + 1)
            def _(h=h):
                for which in range(3):
                    far_copy(which, h).wait_recv()

        def emit(which, i, value):
            acc[which, i] = value + get(1, which, k, i)

            @pl.when(k == (1 if i < per // 2 else 3))
            def _():
                acc[which, i] = acc[which, i] + get(3, which, 2, i)

            @pl.when(k > 0)
            def _():
                put(2, which, k, i, acc[which, i])

        own_grads(target, emit)

        @pl.when(k == 2)
        def _():
            for which in range(3):
                for h in range(2):
                    far_copy(which, h).start()

        @pl.when(lax.rem(k, 2) == 1)
        def _():
            for which in range(3):
                ring_copy(which, k, target).start()

    def to_owners(s, _):
        order = (2, 1, 3, 0)

        @pl.when(s < n_y)
        def _():
            to_sibling(pick(s, order))

        @pl.when(s >= 1)
        def _():
            to_ring(pick(s - 1, order))

        return 0

    def collect(side, _):
        k = 2 * side + 1
        for which in range(3):
            ring_copy(which, k, sibling).wait_recv()
            for i in range(per):
                acc[which, i] = acc[which, i] + get(3, which, k, i)
        return 0

    @pl.when(by_factors)
    def _():
        xnr[c] = xn[pl.ds(c * per, per)]
        send_factors()
        lax.fori_loop(1, n_col, send_xn, 0)

    @pl.when(p == 0)
    def _():
        spread_factors()

    for k in range(AHEAD):
        take_dy(k)

    def step(s, _):
        @pl.when(s < CHUNKS)
        def _():
            @pl.when(s < CHUNKS - AHEAD)
            def _():
                take_dy(s + AHEAD)

            products(s)
            back(s)

        @pl.when(jnp.logical_and(s == spread, jnp.logical_and(by_factors, p > 0)))
        def _():
            spread_factors()

        @pl.when(jnp.logical_and(s >= lead, s < lead + CHUNKS))
        def _():
            pass_on(s - lead)

        @pl.when(jnp.logical_and(s >= lead + 1, s < lead + 1 + CHUNKS))
        def _():
            grads(s - lead - 1)

        @pl.when(jnp.logical_and(s >= lead, s < lead + CHUNKS))
        def _():
            prepare(s - lead)

        @pl.when(jnp.logical_and(s >= late, s < CHUNKS + late))
        def _():
            finish(s - late)

        return 0

    late = jnp.where(p == n_pipe - 1, FIRST_LATE, LATE)
    spread = jnp.where(p == 1, SPREAD, CHUNKS + LATE)
    lead = jnp.where(p == 0, FACTORS_LATE, jnp.where(by_factors, CHUNKS + LATE, 3 * CHUNKS))
    lax.fori_loop(0, 2 * CHUNKS + LATE + 1, step, 0)

    @pl.when(jnp.logical_not(by_factors))
    def _():
        lax.fori_loop(0, n_y + 1, to_owners, 0)
        lax.fori_loop(0, 2, collect, 0)

    for i in range(per):
        for which, (ref, cnt) in enumerate(((ggate_ref, icnt), (gup_ref, icnt), (gdown_ref, ocnt))):
            live = cnt[c * per + i]
            slot = lax.broadcasted_iota(jnp.int32, (BLK, 2 * BLK), 1) // BLK
            ref[i * BLK : (i + 1) * BLK, :] = jnp.where(slot < live, acc[which, i], 0.0).astype(BF16)

    def sent_weights(number, _):
        weights(c, 0, sibling, number).wait_send()
        return 0

    lax.fori_loop(0, 28, sent_weights, 0)

    def sent(d, _):
        other = lax.rem(r + d, n_row)
        x_copy(r, other, d).wait_send()
        for k in range(CHUNKS):
            sum_copy(k, other, r, d).wait_send()
        return 0

    lax.fori_loop(1, n_row, sent, 0)

    def sent_dy(d, _):
        for k in range(CHUNKS):
            dy_copy(k, x, lax.rem(x + d, n_x), d).wait_send()
        return 0

    lax.fori_loop(1, n_x, sent_dy, 0)

    @pl.when(p == n_pipe - 1)
    def _():
        for k in range(CHUNKS):
            swap_copy(k).wait_send()

    @pl.when(p > 0)
    def _():
        for k in range(CHUNKS):
            hop_copy(k, p - 1, r, 0).wait_send()
            hop_copy(k, p - 1, partner, 1).wait_send()

    @pl.when(jnp.logical_not(by_factors))
    def _():
        for which in range(3):
            for k in range(n_y):
                pair_copy(which, k).wait_send()
            for h in range(2):
                far_copy(which, h).wait_send()
                ring_copy(which, 2 * h + 1, sibling).wait_send()

    @pl.when(by_factors)
    def _():
        def sent_beside(d, _):
            beside = lax.rem(c + d, n_col)
            xn_copy(beside, c, d).wait_send()
            for k in range(CHUNKS):
                dyc_copy(k, beside, c, d).wait_send()
            return 0

        lax.fori_loop(1, n_col, sent_beside, 0)

        def sent_factors(number, _):
            factor_copy(c, sibling, number).wait_send()
            for k in range(CHUNKS):
                dh_copy(k, c, sibling, number).wait_send()
            return 0

        lax.fori_loop(0, 2 * n_y - 1, sent_factors, 0)


def hand_over(a, b, c, d, out_a, out_b, out_c, out_d):
    for src, dst in ((a, out_a), (b, out_b), (c, out_c), (d, out_d)):
        dst[...] = src[...]


def local(sizes, inputs, grad_out, norm_gain, gate_weight, up_weight, down_weight, inner_cols, inner_counts, outer_cols, outer_counts):
    n_pipe, n_row, n_y, blocks = sizes
    n_col, n_x = 2 * n_y, n_row // 2
    _, micro, tokens, width = inputs.shape
    both = micro * tokens
    small = both // CHUNKS
    block_rows = width * n_row // BLK
    per = block_rows // n_row
    slots = 2 * block_rows
    rows = gate_weight.shape[1]
    icol, ocol = inner_cols[0].T, outer_cols[0].T
    icnt, ocnt = inner_counts.reshape(block_rows), outer_counts.reshape(block_rows)
    smem = pl.BlockSpec(memory_space=pltpu.SMEM)
    vmem = pl.BlockSpec(memory_space=pltpu.VMEM)
    dma = pltpu.SemaphoreType.DMA
    weight_out = jax.ShapeDtypeStruct((rows, 2 * BLK), BF16)
    outs = (jax.ShapeDtypeStruct((both, width), BF16), weight_out, weight_out, weight_out)
    results = pl.pallas_call(
        functools.partial(main_kernel, sizes),
        out_shape=outs,
        in_specs=[vmem] * 3 + [pl.BlockSpec(memory_space=pl.ANY)] * 3 + [vmem] * 2 + [smem] * 4,
        out_specs=[vmem] * 4,
        scratch_shapes=[
            pltpu.VMEM((n_col, 3 * rows, 2 * BLK), BF16),
            pltpu.VMEM((block_rows, 4 * BLK, BLK), BF16),
            pltpu.VMEM((n_row, both + 16, width), BF16),
            pltpu.VMEM((block_rows, both, BLK), BF16),
            pltpu.VMEM((both, BLK), F32),
            pltpu.VMEM((slots, both, BLK), F32),
            pltpu.VMEM((slots, both, BLK), F32),
            pltpu.VMEM((slots, both, BLK), F32),
            pltpu.VMEM((blocks, both, BLK), F32),
            pltpu.VMEM((blocks, both, BLK), F32),
            pltpu.VMEM((blocks, both, BLK), F32),
            pltpu.VMEM((blocks, both, BLK), BF16),
            pltpu.VMEM((max(n_col * 2 * blocks * both, (12 * n_y - 6) * 2 * rows), BLK), BF16),
            pltpu.VMEM((CHUNKS, n_col, blocks, small, BLK), BF16),
            pltpu.VMEM((blocks, both, BLK), BF16),
            pltpu.VMEM((blocks, both, BLK), BF16),
            pltpu.VMEM((CHUNKS, n_row, small, width), BF16),
            pltpu.VMEM((CHUNKS, n_col, small, width), BF16),
            pltpu.VMEM((n_col, per, both, BLK), BF16),
            pltpu.VMEM((CHUNKS, n_row, small, width + BLK), BF16),
            pltpu.VMEM((CHUNKS, n_row, small, width + BLK), BF16),
            pltpu.VMEM((blocks, n_col * small, BLK), BF16),
            pltpu.VMEM((blocks, n_col * small, BLK), BF16),
            pltpu.VMEM((blocks, n_col * small, BLK), BF16),
            pltpu.VMEM((blocks, n_col * small, BLK), BF16),
            pltpu.VMEM((blocks, n_col * small, BLK), BF16),
            pltpu.VMEM((per, BLK, n_col * small), BF16),
            pltpu.VMEM((3, per, BLK, 2 * BLK), F32),
            pltpu.VMEM((8, BLK), jnp.int32),
            pltpu.SMEM((8, BLK), jnp.int32),
            pltpu.VMEM((3, rows, 2 * BLK), BF16),
            dma((3,)),
            dma,
            dma((28,)), dma((n_col, per)),
            dma((n_row,)), dma((n_row,)),
            dma((CHUNKS, n_x)), dma((CHUNKS, n_x)),
            dma((CHUNKS, 2)), dma((CHUNKS, 2)),
            dma((CHUNKS, n_row)), dma((CHUNKS, n_row)),
            dma((2 * n_y - 1,)), dma((n_col,)),
            dma((n_col,)), dma((n_col,)),
            dma((CHUNKS, 2 * n_y - 1)), dma((CHUNKS, n_col)),
            dma((CHUNKS, n_col)), dma((CHUNKS, n_col)),
            dma((3, n_y)), dma((3, n_y)),
            dma((3, n_y)), dma((3, n_y)),
        ],
        compiler_params=pltpu.CompilerParams(collective_id=0, has_side_effects=True, vmem_limit_bytes=60 * 1024 * 1024),
        name="backward",
    )(
        inputs.reshape(both, width), grad_out.reshape(both, width), norm_gain,
        gate_weight.reshape(rows, 2 * BLK), up_weight.reshape(rows, 2 * BLK), down_weight.reshape(rows, 2 * BLK),
        icol, ocol, icol, icnt, ocol, ocnt,
    )
    grad_in, gate, up, down = pl.pallas_call(
        hand_over,
        out_shape=outs,
        in_specs=[vmem] * 4,
        out_specs=[vmem] * 4,
        name="hand_over",
    )(*results)
    return grad_in.reshape(inputs.shape), gate[None], up[None], down[None]


def solution(mesh):
    in_specs = (
        P("pipe", None, "col", "row"),
        P(None, "col", "row"),
        P("pipe", "row"),
        P("pipe", "col", "row"),
        P("pipe", "col", "row"),
        P("pipe", "col", "row"),
        P("pipe", None, "row"),
        P("pipe", None, "row"),
        P("pipe", None, "row"),
        P("pipe", None, "row"),
    )
    out_specs = (
        P("pipe", None, "col", "row"),
        P("pipe", "col", "row"),
        P("pipe", "col", "row"),
        P("pipe", "col", "row"),
    )
    sizes = (mesh.shape["pipe"], mesh.shape["row"], mesh.shape["col"] // 2, FF // (mesh.shape["row"] * BLK))
    return jax.shard_map(functools.partial(local, sizes), mesh=mesh, in_specs=in_specs, out_specs=out_specs, check_vma=False)
```
